128 devices in a mesh: seq: 32 (over z, y_lo, x), rep: 4 (over y_hi, core).
Axes of the slice: x: 4, y: 4 (y_hi: 2, y_lo: 2; y = y_hi * 2 + y_lo), z: 4, core: 2. Of those that a mesh axis runs over, the one named last changes fastest.
Arguments:
- queries: bfloat16 [4, 32768, 768], P('rep', 'seq'), may hold values from -6 to 6
- key_rows: bfloat16 [4, 32768, 768], P('rep', 'seq'), may hold values from -6 to 6
- value_rows: bfloat16 [4, 32768, 768], P('rep', 'seq'), may hold values from -6 to 6
- saved_out: bfloat16 [4, 32768, 768], P('rep', 'seq'), may hold values from -12 to 12
- logsumexp: float32 [4, 12, 32768], P('rep', None, 'seq'), may hold values from 7 to 8
- out_grad: bfloat16 [4, 32768, 768], P('rep', 'seq'), may hold values from -3 to 3
- proj_weight: bfloat16 [768, 768], replicated, may hold values from -0.21875 to 0.21875
Outputs:
- grad_query: bfloat16 [4, 32768, 768], P('rep', 'seq')
- grad_key: bfloat16 [4, 32768, 768], P('rep', 'seq')
- grad_value: bfloat16 [4, 32768, 768], P('rep', 'seq')
- projection_gradient: float32 [768, 768], P('seq')
The draws below stay inside these ranges and needn't reach their ends.
All inputs are finite; a program needn't handle non-finite values.
Results may differ from the reference program's by a relative error of at most 0.0057.
Values may be sent and summed in bfloat16 or wider, within the bound.
No kernel may reach another device: no remote copies, remote signals or barrier semaphores. Data moves between devices by JAX's collectives and lax.ppermute only.
A program may use at most 128 MiB of HBM per device.

```python
import math
import jax
import jax.numpy as jnp
from jax import lax

HEAD_TOTAL = 12
HEAD_WIDTH = 64
D = 768
TOK_DEV = 1024
DILATION_STEP = 128
TILE_TOKENS = 32768
SLIDES = 4


def raised(drawn, own_key, source, target, blocks, factor):
    def block_of(axis_at):
        return (jnp.arange(drawn.shape[axis_at]) // (drawn.shape[axis_at] // blocks)).reshape((-1,) + (1,) * (drawn.ndim - 1 - axis_at))

    near = jax.random.permutation(own_key, blocks)[block_of(target)]
    second = (block_of(target) + blocks // 2) % blocks
    return jnp.where((block_of(source) == near) | (block_of(source) == second), factor * drawn, drawn)


def steps_of(own_key, extent, shards, smallest, largest):
    loudness, own = 1.0, jax.random.fold_in(own_key, 6)
    for axis_at, parts in shards:
        draws = jnp.exp(jax.random.uniform(jax.random.fold_in(own, axis_at), (parts,), jnp.float32, smallest / len(shards), largest / len(shards)))
        loudness = loudness * jnp.repeat(draws, extent[axis_at] // parts).reshape([-1 if axis == axis_at else 1 for axis in range(len(extent))])
    return loudness


def centred(own_key, dims, scale, most, cuts=(), held_as=jnp.bfloat16):
    result = jax.random.normal(own_key, dims, jnp.float32) * scale
    if len(cuts) > 0:
        result = steps_of(own_key, dims, cuts, -0.22, 0.18) * result
    return jnp.clip(result, min=-most, max=most).astype(held_as)


def gaussian_with(stream_key, shape, scale, most, cuts, heavy, kind=jnp.bfloat16):
    array = scale * jax.random.normal(stream_key, shape, jnp.float32)
    if cuts:
        array = array * steps_of(stream_key, shape, cuts, -0.22, 0.18)
    return jnp.clip(raised(array, jax.random.fold_in(stream_key, 3), *heavy), -most, most).astype(kind)


def setup_inputs(seed: int = 0) -> dict:
    key_of = jax.random.split(jax.random.key(seed), 8)
    return {
        "queries": centred(key_of[0], (SLIDES, TILE_TOKENS, D), 1.0, 6.0, ((0, 4), (1, 32))),
        "key_rows": centred(key_of[1], (SLIDES, TILE_TOKENS, D), 1.0, 6.0, ((0, 4), (1, 32))),
        "value_rows": centred(key_of[2], (SLIDES, TILE_TOKENS, D), 1.0, 6.0, ((0, 4), (1, 32))),
        "saved_out": gaussian_with(key_of[3], (SLIDES, TILE_TOKENS, D), 1.0, 12.0, ((0, 4), (1, 32)), (1, 2, 32, 2.75)),
        "logsumexp": jnp.clip(7.0 + 1.0 * jax.random.uniform(key_of[4], (SLIDES, HEAD_TOTAL, TILE_TOKENS), jnp.float32) ** steps_of(key_of[4], (SLIDES, HEAD_TOTAL, TILE_TOKENS), ((0, 4), (2, 32)), -0.2, 0.2), 7.0, 8.0),
        "out_grad": centred(key_of[5], (SLIDES, TILE_TOKENS, D), 0.5, 3.0, ((0, 4), (1, 32))),
        "proj_weight": centred(key_of[6], (D, D), D ** -0.5, 0.21875),
    }


def attend_heads(query_tensor, key_tensor, value_tensor, grad3, lse_rows, delta_rows):
    scaling = HEAD_WIDTH ** (-0.5)
    query_f = query_tensor.astype(jnp.float32)
    key_f = key_tensor.astype(jnp.float32)
    value_f = value_tensor.astype(jnp.float32)
    grad_f = grad3.astype(jnp.float32)
    score_matrix = jnp.einsum('thd,uhd->htu', query_f, key_f) * scaling
    probability = jnp.exp(score_matrix - lse_rows[:, :, None])
    probs_gradient = jnp.einsum('thd,uhd->htu', grad_f, value_f)
    scores_gradient = lax.optimization_barrier((probability * (probs_gradient - delta_rows.T[:, :, None])).astype(jnp.bfloat16)).astype(jnp.float32)
    weight_matrix = lax.optimization_barrier(probability.astype(jnp.bfloat16)).astype(jnp.float32)
    query_gradient = jnp.einsum('htu,uhd->thd', scores_gradient, key_f) * scaling
    grad_k = jnp.einsum('htu,thd->uhd', scores_gradient, query_f) * scaling
    value_gradient = jnp.einsum('htu,thd->uhd', weight_matrix, grad_f)
    return (query_gradient, grad_k, value_gradient)

def reference(queries, key_rows, value_rows, saved_out, logsumexp, out_grad, proj_weight):
    segments = TILE_TOKENS // TOK_DEV
    dilated_count = TILE_TOKENS // DILATION_STEP
    index_rows = jnp.arange(HEAD_TOTAL)

    def one_slide(inputs):
        query_mat, key_mat, value_mat, saved_mat, logsum_matrix, grad_mat = inputs
        attn_grad = lax.dot_general(grad_mat, proj_weight, (((1,), (1,)), ((), ())), preferred_element_type=jnp.float32).astype(jnp.bfloat16)
        query_tensor = query_mat.reshape(TILE_TOKENS, HEAD_TOTAL, HEAD_WIDTH)
        key_tensor = key_mat.reshape(TILE_TOKENS, HEAD_TOTAL, HEAD_WIDTH)
        value_tensor = value_mat.reshape(TILE_TOKENS, HEAD_TOTAL, HEAD_WIDTH)
        attention_output = attn_grad.reshape(TILE_TOKENS, HEAD_TOTAL, HEAD_WIDTH)
        saved3 = saved_mat.reshape(TILE_TOKENS, HEAD_TOTAL, HEAD_WIDTH)
        delta_value = lax.optimization_barrier(jnp.sum(attention_output.astype(jnp.float32) * saved3.astype(jnp.float32), axis=2))

        def by_segment(array_input):
            return array_input.reshape(segments, TOK_DEV, HEAD_TOTAL, HEAD_WIDTH)

        def one_segment(pieces):
            return attend_heads(*pieces)
        local_branch = lax.map(one_segment, (by_segment(query_tensor), by_segment(key_tensor), by_segment(value_tensor), by_segment(attention_output), logsum_matrix.reshape(HEAD_TOTAL, segments, TOK_DEV).transpose(1, 0, 2), delta_value.reshape(segments, TOK_DEV, HEAD_TOTAL)))

        def pick_rows(array_input):
            return array_input.reshape(dilated_count, DILATION_STEP, HEAD_TOTAL, HEAD_WIDTH)[:, index_rows, index_rows]
        dilated_branch = attend_heads(pick_rows(query_tensor), pick_rows(key_tensor), pick_rows(value_tensor), pick_rows(attention_output), logsum_matrix.reshape(HEAD_TOTAL, dilated_count, DILATION_STEP)[index_rows, :, index_rows], delta_value.reshape(dilated_count, DILATION_STEP, HEAD_TOTAL)[:, index_rows, index_rows])

        def place_rows(array_input):
            full_sequence = jnp.zeros((dilated_count, DILATION_STEP, HEAD_TOTAL, HEAD_WIDTH), jnp.float32).at[:, index_rows, index_rows].set(array_input)
            return full_sequence.reshape(TILE_TOKENS, HEAD_TOTAL, HEAD_WIDTH)
        outputs = []
        for local_level, dilated_level in zip(local_branch, dilated_branch):
            total_sum = local_level.reshape(TILE_TOKENS, HEAD_TOTAL, HEAD_WIDTH) + place_rows(dilated_level)
            outputs.append(total_sum.astype(jnp.bfloat16).reshape(TILE_TOKENS, HEAD_TOTAL * HEAD_WIDTH))
        weight_term = lax.dot_general(saved_mat, grad_mat, (((0,), (0,)), ((), ())), preferred_element_type=jnp.float32)
        return (outputs[0], outputs[1], outputs[2], weight_term)
    grad_query, grad_key, grad_value, weight_terms = lax.map(one_slide, (queries, key_rows, value_rows, saved_out, logsumexp, out_grad))
    projection_gradient = lax.optimization_barrier(jnp.sum(weight_terms, axis=0)) * (1.0 / math.sqrt(SLIDES * TILE_TOKENS))
    return (grad_query, grad_key, grad_value, projection_gradient)
```

```python
import functools
import math

import jax
import jax.numpy as jnp
from jax import lax
from jax.experimental import pallas as pl
from jax.experimental.pallas import tpu as pltpu
from jax.sharding import PartitionSpec as P

F32 = jnp.float32
BF16 = jnp.bfloat16
DIL = 128
HEADS = 12
HW = 64
D = HEADS * HW
SUB = 16
LOG2E = math.log2(math.e)
SCALE = HW ** -0.5
STAT = 2 * D
PROJ = STAT + 128
VMEM = 60 * 2 ** 20


def dot(a, b, ca, cb):
    return lax.dot_general(a, b, (((ca,), (cb,)), ((), ())), preferred_element_type=F32)


def iota(shape, axis):
    return lax.broadcasted_iota(jnp.int32, shape, axis)


def head_rows(rows):
    keep = iota((1, SUB, D), 1) == iota((1, SUB, D), 2) // HW
    return jnp.sum(jnp.where(keep, rows.astype(F32), 0.0), axis=1)


def three_terms(x):
    x = jnp.where(iota(x.shape, 1) < HEADS, x, 0.0)
    hi = x.astype(BF16).astype(F32)
    mid = (x - hi).astype(BF16).astype(F32)
    low = ((x - hi) - mid).astype(BF16).astype(F32)
    return hi + pltpu.roll(mid, 16, 1) + pltpu.roll(low, 32, 1)


def join_terms(x):
    return (x + pltpu.roll(x, 112, 1)) + pltpu.roll(x, 96, 1)


def front_kernel(steps, seq, saved_ref, grad_ref, w_ref, lse_ref, q_ref, k_ref, v_ref,
                 attn_ref, delta_ref, send_ref, acc, gsel, dsel):
    step = pl.program_id(0)
    saved = saved_ref[...]
    grad = grad_ref[...]
    rows = saved.shape[0]
    attn = dot(grad, w_ref[...], 1, 1).astype(BF16)
    attn_ref[...] = attn
    attn_f = attn.astype(F32)
    term = dot(saved, grad, 0, 0)

    @pl.when(step == 0)
    def _():
        acc[...] = term

    @pl.when(step > 0)
    def _():
        acc[...] += term

    prod = attn_f * saved.astype(F32)
    hi = prod.astype(BF16)
    low = (prod - hi.astype(F32)).astype(BF16)
    pick = (iota((D, 128), 0) // HW == iota((D, 128), 1)).astype(BF16)
    delta = dot(hi, pick, 1, 0) + dot(low, pick, 1, 0)
    delta_ref[...] = delta.T[:SUB]
    groups = rows // DIL
    grouped = attn_f.reshape(groups, DIL, D)[:, :SUB]
    picked = head_rows(grouped)
    diag = iota((1, DIL, 128), 1) == iota((1, DIL, 128), 2)
    dpicked = jnp.sum(jnp.where(diag, delta.reshape(groups, DIL, 128), 0.0), axis=1)
    for i in range(groups):
        gsel[pl.ds(step * groups + i, 1), :] = picked[i:i + 1]
        dsel[pl.ds(step * groups + i, 1), :] = dpicked[i:i + 1]

    @pl.when(step == steps - 1)
    def _():
        diag = iota((HEADS, 128), 0) == iota((HEADS, 128), 1)
        lse = jnp.concatenate(
            [jnp.sum(jnp.where(diag, lse_ref[:, DIL * j:DIL * (j + 1)], 0.0), axis=0, keepdims=True)
             for j in range(8)], axis=0)
        top = jnp.concatenate([head_rows(q_ref[...]), head_rows(k_ref[...]), three_terms(lse)], axis=1)
        bot = jnp.concatenate([head_rows(v_ref[...]), gsel[...], three_terms(dsel[...])], axis=1)
        own = jnp.concatenate([top, bot], axis=0).astype(BF16)
        share = D // seq
        for s in range(seq):
            send_ref[s, :, 0:PROJ] = own
            send_ref[s, :, PROJ:PROJ + D] = acc[share * s:share * s + 16].astype(BF16)
            rest = acc[share * s + 16:share * s + 24]
            send_ref[s, :, PROJ + D:PROJ + D + D // 2] = jnp.concatenate(
                [rest[:, :D // 2], rest[:, D // 2:]], axis=0).astype(BF16)


def front(saved, grad, w, lse, q, k, v, seq):
    tok = saved.shape[0]
    steps = 4
    rows = tok // steps
    row_spec = pl.BlockSpec((rows, D), lambda i: (i, 0))
    sel_spec = pl.BlockSpec((tok // DIL, SUB, D), lambda i: (0, 0, 0))
    view = lambda x: x.reshape(tok // DIL, DIL, D)
    return pl.pallas_call(
        functools.partial(front_kernel, steps, seq),
        grid=(steps,),
        in_specs=[row_spec, row_spec,
                  pl.BlockSpec((D, D), lambda i: (0, 0)),
                  pl.BlockSpec((HEADS, tok), lambda i: (0, 0)),
                  sel_spec, sel_spec, sel_spec],
        out_specs=[row_spec,
                   pl.BlockSpec((SUB, rows), lambda i: (0, i)),
                   pl.BlockSpec((seq, 16, PROJ + D + D // 2), lambda i: (0, 0, 0))],
        out_shape=[jax.ShapeDtypeStruct((tok, D), BF16),
                   jax.ShapeDtypeStruct((SUB, tok), F32),
                   jax.ShapeDtypeStruct((seq, 16, PROJ + D + D // 2), BF16)],
        scratch_shapes=[pltpu.VMEM((D, D), F32),
                        pltpu.VMEM((tok // DIL, D), F32),
                        pltpu.VMEM((tok // DIL, 128), F32)],
        compiler_params=pltpu.CompilerParams(vmem_limit_bytes=VMEM),
        cost_estimate=pl.CostEstimate(flops=4 * tok * D * D, bytes_accessed=9 * 10 ** 6, transcendentals=0),
    )(saved, grad, w, lse, view(q), view(k), view(v))


def local_kernel(chunk, q_ref, k_ref, v_ref, g_ref, lse_ref, delta_ref,
                 dq_ref, dk_ref, dv_ref, sq_ref, sk_ref, sv_ref):
    pair = pl.program_id(0)
    q2, k2, v2, g2 = q_ref[...], k_ref[...], v_ref[...], g_ref[...]
    tok = q2.shape[0]
    lane = iota((1, 128), 1)
    k_turned = k2.T
    zero = jnp.zeros((), BF16)
    qm = [jnp.where(lane < HW, q2, zero), jnp.where(lane >= HW, q2, zero)]
    gm = [jnp.where(lane < HW, g2, zero), jnp.where(lane >= HW, g2, zero)]
    grad_k = grad_v = None
    grad_q = []
    for c in range(tok // chunk):
        part = slice(c * chunk, (c + 1) * chunk)
        turned = []
        for h in range(2):
            qc, gc = qm[h][part], gm[h][part]
            lse = lse_ref[pl.ds(2 * pair + h, 1), part] * LOG2E
            delta = delta_ref[pl.ds(2 * pair + h, 1), part]
            prob = jnp.exp2(dot(k2, qc, 1, 1) * (SCALE * LOG2E) - lse)
            dscore = (prob * (dot(v2, gc, 1, 1) - delta)).astype(BF16)
            weight = prob.astype(BF16)
            a, b = dot(dscore, qc, 1, 0), dot(weight, gc, 1, 0)
            grad_k = a if grad_k is None else grad_k + a
            grad_v = b if grad_v is None else grad_v + b
            turned.append(dot(k_turned[HW * h:HW * h + HW], dscore, 1, 0))
        grad_q.append(jnp.concatenate(turned, axis=0).T)
    grad_q = jnp.concatenate(grad_q, axis=0) * SCALE
    grad_k = grad_k * SCALE
    groups = tok // DIL
    keep = iota((1, DIL, 128), 1) == 2 * pair + iota((1, DIL, 128), 2) // HW
    for out, sel, val in ((dq_ref, sq_ref, grad_q), (dk_ref, sk_ref, grad_k), (dv_ref, sv_ref, grad_v)):
        out[...] = val.astype(BF16)
        sel[...] = jnp.sum(jnp.where(keep, val.reshape(groups, DIL, 128), 0.0), axis=1)


def local_level(q, k, v, g, lse, delta):
    tok = q.shape[0]
    pairs = HEADS // 2
    col = pl.BlockSpec((tok, 128), lambda i: (0, i))
    sel = pl.BlockSpec((tok // DIL, 128), lambda i: (0, i))
    return pl.pallas_call(
        functools.partial(local_kernel, 256),
        grid=(pairs,),
        in_specs=[col] * 4 + [pl.BlockSpec((HEADS, tok), lambda i: (0, 0)),
                              pl.BlockSpec((SUB, tok), lambda i: (0, 0))],
        out_specs=[col] * 3 + [sel] * 3,
        out_shape=[jax.ShapeDtypeStruct((tok, D), BF16)] * 3
        + [jax.ShapeDtypeStruct((tok // DIL, D), F32)] * 3,
        compiler_params=pltpu.CompilerParams(vmem_limit_bytes=VMEM),
        cost_estimate=pl.CostEstimate(flops=10 * HEADS * tok * tok * HW * 2, bytes_accessed=11 * 10 ** 6,
                                      transcendentals=HEADS * tok * tok),
    )(q, k, v, g, lse, delta)


def last_kernel(recv_ref, own_ref, sq_ref, sk_ref, sv_ref, dq_in, dk_in, dv_in, dq_ref, dk_ref, dv_ref):
    every = recv_ref[...].astype(F32)
    count = every.shape[0] * 8
    top = every[:, :8].reshape(count, PROJ)
    bot = every[:, 8:].reshape(count, PROJ)
    q, k = top[:, :D].astype(BF16), top[:, D:2 * D].astype(BF16)
    v, g = bot[:, :D].astype(BF16), bot[:, D:2 * D].astype(BF16)
    lse = join_terms(top[:, STAT:]).T[:HEADS]
    delta = join_terms(bot[:, STAT:]).T[:HEADS]
    own = own_ref[0].astype(F32)
    own_head = iota((HEADS, 8, D), 0) == iota((HEADS, 8, D), 2) // HW

    def by_head(x):
        return jnp.where(own_head, jnp.broadcast_to(x[None], (HEADS, 8, D)), 0.0).reshape(HEADS * 8, D).astype(BF16)

    def column(x):
        x = jnp.broadcast_to(join_terms(x)[None], (HEADS, 8, 128))
        x = jnp.where(iota(x.shape, 0) == iota(x.shape, 2), x, 0.0)
        return jnp.sum(x.reshape(HEADS * 8, 128), axis=1, keepdims=True)

    def row(x):
        return jnp.broadcast_to(x[:, None], (HEADS, 8, count)).reshape(HEADS * 8, count)

    def back(x):
        return jnp.sum(jnp.where(own_head, x.reshape(HEADS, 8, D), 0.0), axis=0)

    def pieces(left_s, right_s, left_p, right_p, lse, delta):
        prob = jnp.exp2(dot(left_s, right_s, 1, 1) * (SCALE * LOG2E) - lse * LOG2E)
        dscore = (prob * (dot(left_p, right_p, 1, 1) - delta)).astype(BF16)
        return prob.astype(BF16), dscore

    _, dscore = pieces(by_head(own[:8, :D]), k, by_head(own[8:, D:2 * D]), v,
                       column(own[:8, STAT:]), column(own[8:, STAT:]))
    grad_q = back(dot(dscore, k, 1, 0)) * SCALE
    weight, dscore = pieces(by_head(own[:8, D:2 * D]), q, by_head(own[8:, :D]), g, row(lse), row(delta))
    grad_k = back(dot(dscore, q, 1, 0)) * SCALE
    grad_v = back(dot(weight, g, 1, 0))
    here = iota((8, SUB, D), 1) == iota((8, SUB, D), 2) // HW
    for sel, grad, old, out in ((sq_ref, grad_q, dq_in, dq_ref), (sk_ref, grad_k, dk_in, dk_ref),
                                (sv_ref, grad_v, dv_in, dv_ref)):
        total = sel[...] + grad
        out[...] = jnp.where(here, jnp.broadcast_to(total[:, None], (8, SUB, D)),
                             old[...].astype(F32)).astype(BF16)


def last(recv, send, sums, grads):
    seq = recv.shape[0]
    tok = grads[0].shape[0]
    sub = pl.BlockSpec((tok // DIL, SUB, D), lambda i: (0, 0, 0))
    sel = pl.BlockSpec((tok // DIL, D), lambda i: (0, 0))
    view = jax.ShapeDtypeStruct((tok // DIL, DIL, D), BF16)
    return pl.pallas_call(
        last_kernel,
        grid=(1,),
        in_specs=[pl.BlockSpec((seq, 16, PROJ), lambda i: (0, 0, 0)),
                  pl.BlockSpec((1, 16, PROJ), lambda i: (0, 0, 0))] + [sel] * 3 + [sub] * 3,
        out_specs=[sub] * 3,
        out_shape=[view] * 3,
        input_output_aliases={5: 0, 6: 1, 7: 2},
        compiler_params=pltpu.CompilerParams(vmem_limit_bytes=VMEM),
        cost_estimate=pl.CostEstimate(flops=7 * 2 * 96 * 256 * D, bytes_accessed=4 * 10 ** 6,
                                      transcendentals=2 * 96 * 256),
    )(recv, send, *sums, *[x.reshape(view.shape) for x in grads])


def on_device(queries, key_rows, value_rows, saved_out, logsumexp, out_grad, proj_weight):
    q, k, v = queries[0], key_rows[0], value_rows[0]
    lse = logsumexp[0]
    tok = q.shape[0]
    seq = lax.axis_size("seq")
    rep = lax.axis_size("rep")
    attn, delta, send = front(saved_out[0], out_grad[0], proj_weight, lse, q, k, v, seq)
    recv = lax.all_to_all(send, "seq", 0, 0)
    *grads, sq, sk, sv = local_level(q, k, v, attn, lse, delta)
    total = jnp.sum(recv[:, :, PROJ:].astype(F32), axis=0)
    rest = total[:, D:]
    mine = jnp.concatenate([total[:, :D], jnp.concatenate([rest[:8], rest[8:]], axis=1)], axis=0)

    def other(x, bit):
        return lax.ppermute(x, "rep", [(i, i ^ bit) for i in range(rep)])

    pair_sum = mine + other(mine, 2)
    all_sum = pair_sum + other(pair_sum, 1)
    projection_gradient = all_sum * (1.0 / math.sqrt(rep * seq * tok))
    outs = last(recv, send, (sq, sk, sv), grads)
    return (*[x.reshape(1, tok, D) for x in outs], projection_gradient)


def solution(mesh):
    rows = P("rep", "seq", None)
    return jax.shard_map(
        on_device,
        mesh=mesh,
        in_specs=(rows, rows, rows, rows, P("rep", None, "seq"), rows, P()),
        out_specs=(rows, rows, rows, P("seq", None)),
        check_vma=False,
    )
```

```python
import functools
import math

import jax
import jax.numpy as jnp
from jax import lax
from jax.experimental import pallas as pl
from jax.experimental.pallas import tpu as pltpu
from jax.sharding import PartitionSpec as P

F32 = jnp.float32
BF16 = jnp.bfloat16
DIL = 128
HEADS = 12
HW = 64
D = HEADS * HW
SUB = 16
LOG2E = math.log2(math.e)
SCALE = HW ** -0.5
STAT = 2 * D
PROJ = STAT + 128
TERM = D + D // 2
VMEM = 62 * 2 ** 20


def dot(a, b, ca, cb):
    return lax.dot_general(a, b, (((ca,), (cb,)), ((), ())), preferred_element_type=F32)


def iota(shape, axis):
    return lax.broadcasted_iota(jnp.int32, shape, axis)


def head_rows(rows):
    keep = iota((1, SUB, D), 1) == iota((1, SUB, D), 2) // HW
    return jnp.sum(jnp.where(keep, rows.astype(F32), 0.0), axis=1)


def three_terms(x):
    x = jnp.where(iota(x.shape, 1) < HEADS, x, 0.0)
    hi = x.astype(BF16).astype(F32)
    mid = (x - hi).astype(BF16).astype(F32)
    low = ((x - hi) - mid).astype(BF16).astype(F32)
    return hi + pltpu.roll(mid, 16, 1) + pltpu.roll(low, 32, 1)


def join_terms(x):
    return (x + pltpu.roll(x, 112, 1)) + pltpu.roll(x, 96, 1)


def front_kernel(steps, seq, saved_ref, grad_ref, w_ref, lse_ref, q_ref, k_ref, v_ref,
                 attn_ref, delta_ref, send_ref, acc, gsel, dsel):
    step = pl.program_id(0)
    saved = saved_ref[...]
    grad = grad_ref[...]
    rows = saved.shape[0]
    attn = dot(grad, w_ref[...], 1, 1).astype(BF16)
    attn_ref[...] = attn
    attn_f = attn.astype(F32)
    term = dot(saved, grad, 0, 0)

    @pl.when(step == 0)
    def _():
        acc[...] = term

    @pl.when(step > 0)
    def _():
        acc[...] += term

    prod = attn_f * saved.astype(F32)
    hi = prod.astype(BF16)
    low = (prod - hi.astype(F32)).astype(BF16)
    pick = (iota((D, 128), 0) // HW == iota((D, 128), 1)).astype(BF16)
    delta = dot(hi, pick, 1, 0) + dot(low, pick, 1, 0)
    delta_ref[...] = delta.T[:SUB]
    groups = rows // DIL
    grouped = attn_f.reshape(groups, DIL, D)[:, :SUB]
    picked = head_rows(grouped)
    diag = iota((1, DIL, 128), 1) == iota((1, DIL, 128), 2)
    dpicked = jnp.sum(jnp.where(diag, delta.reshape(groups, DIL, 128), 0.0), axis=1)
    for i in range(groups):
        gsel[pl.ds(step * groups + i, 1), :] = picked[i:i + 1]
        dsel[pl.ds(step * groups + i, 1), :] = dpicked[i:i + 1]

    @pl.when(step == steps - 1)
    def _():
        lane = iota((1, 128), 1)
        lse = jnp.concatenate(
            [sum(jnp.where(lane == h, lse_ref[h, :, DIL * j:DIL * (j + 1)], 0.0) for h in range(HEADS))
             for j in range(8)], axis=0)
        top = jnp.concatenate([head_rows(q_ref[...]), head_rows(k_ref[...]), three_terms(lse)], axis=1)
        bot = jnp.concatenate([head_rows(v_ref[...]), gsel[...], three_terms(dsel[...])], axis=1)
        own = jnp.concatenate([top, bot], axis=0).astype(BF16)
        share = D // seq
        for s in range(seq):
            send_ref[s, :, 0:PROJ] = own
            send_ref[s, :, PROJ:PROJ + D] = acc[share * s:share * s + 16].astype(BF16)
            rest = acc[share * s + 16:share * s + 24]
            send_ref[s, :, PROJ + D:] = jnp.concatenate(
                [rest[:, :D // 2], rest[:, D // 2:]], axis=0).astype(BF16)


def front(saved, grad, w, lse, q, k, v, seq):
    tok = saved.shape[0]
    steps = 4
    rows = tok // steps
    row_spec = pl.BlockSpec((rows, D), lambda i: (i, 0))
    sel_spec = pl.BlockSpec((tok // DIL, SUB, D), lambda i: (0, 0, 0))
    view = lambda x: x.reshape(tok // DIL, DIL, D)
    return pl.pallas_call(
        functools.partial(front_kernel, steps, seq),
        grid=(steps,),
        in_specs=[row_spec, row_spec,
                  pl.BlockSpec((D, D), lambda i: (0, 0)),
                  pl.BlockSpec((HEADS, 1, tok), lambda i: (0, 0, 0)),
                  sel_spec, sel_spec, sel_spec],
        out_specs=[row_spec,
                   pl.BlockSpec((SUB, rows), lambda i: (0, i)),
                   pl.BlockSpec((seq, 16, PROJ + TERM), lambda i: (0, 0, 0))],
        out_shape=[jax.ShapeDtypeStruct((tok, D), BF16),
                   jax.ShapeDtypeStruct((SUB, tok), F32),
                   jax.ShapeDtypeStruct((seq, 16, PROJ + TERM), BF16)],
        scratch_shapes=[pltpu.VMEM((D, D), F32),
                        pltpu.VMEM((tok // DIL, D), F32),
                        pltpu.VMEM((tok // DIL, 128), F32)],
        compiler_params=pltpu.CompilerParams(vmem_limit_bytes=VMEM),
        cost_estimate=pl.CostEstimate(flops=4 * tok * D * D, bytes_accessed=9 * 10 ** 6, transcendentals=0),
    )(saved, grad, w, lse, view(q), view(k), view(v))


def local_kernel(chunk, first, q_ref, k_ref, v_ref, g_ref, lse_ref, delta_ref, *rest):
    dq_ref, dk_ref, dv_ref, sq_ref, sk_ref, sv_ref = rest[-6:]
    pair = first + pl.program_id(0)
    q2, k2, v2, g2 = q_ref[...], k_ref[...], v_ref[...], g_ref[...]
    tok = q2.shape[0]
    lane = iota((1, 128), 1)
    k_turned = k2.T
    zero = jnp.zeros((), BF16)
    qm = [jnp.where(lane < HW, q2, zero), jnp.where(lane >= HW, q2, zero)]
    gm = [jnp.where(lane < HW, g2, zero), jnp.where(lane >= HW, g2, zero)]
    grad_k = grad_v = None
    grad_q = []
    for c in range(tok // chunk):
        part = slice(c * chunk, (c + 1) * chunk)
        turned = []
        for h in range(2):
            qc, gc = qm[h][part], gm[h][part]
            lse = lse_ref[2 * pair + h, :, part] * LOG2E
            delta = delta_ref[pl.ds(2 * pair + h, 1), part]
            prob = jnp.exp2(dot(k2, qc, 1, 1) * (SCALE * LOG2E) - lse)
            dscore = (prob * (dot(v2, gc, 1, 1) - delta)).astype(BF16)
            weight = prob.astype(BF16)
            a, b = dot(dscore, qc, 1, 0), dot(weight, gc, 1, 0)
            grad_k = a if grad_k is None else grad_k + a
            grad_v = b if grad_v is None else grad_v + b
            turned.append(dot(k_turned[HW * h:HW * h + HW], dscore, 1, 0))
        grad_q.append(jnp.concatenate(turned, axis=0).T)
    grad_q = jnp.concatenate(grad_q, axis=0) * SCALE
    grad_k = grad_k * SCALE
    groups = tok // DIL
    keep = iota((1, DIL, 128), 1) == 2 * pair + iota((1, DIL, 128), 2) // HW
    for out, sel, val in ((dq_ref, sq_ref, grad_q), (dk_ref, sk_ref, grad_k), (dv_ref, sv_ref, grad_v)):
        out[...] = val.astype(BF16)
        sel[...] = jnp.sum(jnp.where(keep, val.reshape(groups, DIL, 128), 0.0), axis=1)


def local_level(first, count, q, k, v, g, lse, delta, before=(), after=None):
    tok = q.shape[0]
    col = pl.BlockSpec((tok, 128), lambda i: (0, first + i))
    sel = pl.BlockSpec((tok // DIL, 128), lambda i: (0, first + i))
    extra = list(before) + ([] if after is None else [after])
    return pl.pallas_call(
        functools.partial(local_kernel, 256, first),
        grid=(count,),
        in_specs=[col] * 4 + [pl.BlockSpec((HEADS, 1, tok), lambda i: (0, 0, 0)),
                              pl.BlockSpec((SUB, tok), lambda i: (0, 0))]
        + [pl.BlockSpec(memory_space=pl.ANY)] * len(extra),
        out_specs=[col] * 3 + [sel] * 3,
        out_shape=[jax.ShapeDtypeStruct((tok, D), BF16)] * 3
        + [jax.ShapeDtypeStruct((tok // DIL, D), F32)] * 3,
        input_output_aliases={6 + i: i for i in range(len(before))},
        compiler_params=pltpu.CompilerParams(vmem_limit_bytes=VMEM),
        cost_estimate=pl.CostEstimate(flops=20 * count * tok * tok * HW * 2, bytes_accessed=2 * count * 10 ** 6,
                                      transcendentals=2 * count * tok * tok),
    )(q, k, v, g, lse, delta, *extra)


def add_kernel(a_ref, b_ref, after, out_ref):
    out_ref[...] = a_ref[...] + b_ref[...]


def add_after(a, b, after):
    whole = pl.BlockSpec(a.shape, lambda: (0, 0))
    return pl.pallas_call(
        add_kernel,
        in_specs=[whole, whole, pl.BlockSpec(memory_space=pl.ANY)],
        out_specs=whole,
        out_shape=jax.ShapeDtypeStruct(a.shape, a.dtype),
        cost_estimate=pl.CostEstimate(flops=a.size, bytes_accessed=12 * a.size, transcendentals=0),
    )(a, b, after)


def terms_kernel(recv_ref, after, out_ref):
    total = jnp.sum(recv_ref[...].astype(F32), axis=0)
    out_ref[:16] = total[:, :D]
    out_ref[16:, :D // 2] = total[:8, D:]
    out_ref[16:, D // 2:] = total[8:, D:]


def sum_terms(recv, after):
    seq = recv.shape[0]
    return pl.pallas_call(
        terms_kernel,
        grid=(1,),
        in_specs=[pl.BlockSpec((pl.Element(seq), pl.Element(16), pl.Element(TERM)), lambda i: (0, 0, PROJ)),
                  pl.BlockSpec(memory_space=pl.ANY)],
        out_specs=pl.BlockSpec((24, D), lambda i: (0, 0)),
        out_shape=jax.ShapeDtypeStruct((24, D), F32),
        compiler_params=pltpu.CompilerParams(vmem_limit_bytes=VMEM),
        cost_estimate=pl.CostEstimate(flops=seq * 24 * D, bytes_accessed=10 ** 6, transcendentals=0),
    )(recv, after)


def last_kernel(recv_ref, own_ref, sq_ref, sk_ref, sv_ref, dq_in, dk_in, dv_in, after, dq_ref, dk_ref, dv_ref):
    every = recv_ref[...].astype(F32)
    count = every.shape[0] * 8
    top = every[:, :8].reshape(count, PROJ)
    bot = every[:, 8:].reshape(count, PROJ)
    q, k = top[:, :D].astype(BF16), top[:, D:2 * D].astype(BF16)
    v, g = bot[:, :D].astype(BF16), bot[:, D:2 * D].astype(BF16)
    lse = join_terms(top[:, STAT:]).T[:HEADS]
    delta = join_terms(bot[:, STAT:]).T[:HEADS]
    own = own_ref[0].astype(F32)
    own_head = iota((HEADS, 8, D), 0) == iota((HEADS, 8, D), 2) // HW

    def by_head(x):
        return jnp.where(own_head, jnp.broadcast_to(x[None], (HEADS, 8, D)), 0.0).reshape(HEADS * 8, D).astype(BF16)

    def column(x):
        x = jnp.broadcast_to(join_terms(x)[None], (HEADS, 8, 128))
        x = jnp.where(iota(x.shape, 0) == iota(x.shape, 2), x, 0.0)
        return jnp.sum(x.reshape(HEADS * 8, 128), axis=1, keepdims=True)

    def row(x):
        return jnp.broadcast_to(x[:, None], (HEADS, 8, count)).reshape(HEADS * 8, count)

    def back(x):
        return jnp.sum(jnp.where(own_head, x.reshape(HEADS, 8, D), 0.0), axis=0)

    def pieces(left_s, right_s, left_p, right_p, lse, delta):
        prob = jnp.exp2(dot(left_s, right_s, 1, 1) * (SCALE * LOG2E) - lse * LOG2E)
        dscore = (prob * (dot(left_p, right_p, 1, 1) - delta)).astype(BF16)
        return prob.astype(BF16), dscore

    _, dscore = pieces(by_head(own[:8, :D]), k, by_head(own[8:, D:2 * D]), v,
                       column(own[:8, STAT:]), column(own[8:, STAT:]))
    grad_q = back(dot(dscore, k, 1, 0)) * SCALE
    weight, dscore = pieces(by_head(own[:8, D:2 * D]), q, by_head(own[8:, :D]), g, row(lse), row(delta))
    grad_k = back(dot(dscore, q, 1, 0)) * SCALE
    grad_v = back(dot(weight, g, 1, 0))
    here = iota((8, SUB, D), 1) == iota((8, SUB, D), 2) // HW
    for sel, grad, old, out in ((sq_ref, grad_q, dq_in, dq_ref), (sk_ref, grad_k, dk_in, dk_ref),
                                (sv_ref, grad_v, dv_in, dv_ref)):
        total = sel[...] + grad
        out[...] = jnp.where(here, jnp.broadcast_to(total[:, None], (8, SUB, D)),
                             old[...].astype(F32)).astype(BF16)


def last(recv, send, sums, grads, after):
    seq = recv.shape[0]
    tok = grads[0].shape[0]
    sub = pl.BlockSpec((tok // DIL, SUB, D), lambda i: (0, 0, 0))
    sel = pl.BlockSpec((tok // DIL, D), lambda i: (0, 0))
    view = jax.ShapeDtypeStruct((tok // DIL, DIL, D), BF16)
    return pl.pallas_call(
        last_kernel,
        grid=(1,),
        in_specs=[pl.BlockSpec((seq, 16, PROJ), lambda i: (0, 0, 0)),
                  pl.BlockSpec((1, 16, PROJ), lambda i: (0, 0, 0))] + [sel] * 3 + [sub] * 3
        + [pl.BlockSpec(memory_space=pl.ANY)],
        out_specs=[sub] * 3,
        out_shape=[view] * 3,
        input_output_aliases={5: 0, 6: 1, 7: 2},
        compiler_params=pltpu.CompilerParams(vmem_limit_bytes=VMEM),
        cost_estimate=pl.CostEstimate(flops=7 * 2 * 96 * 256 * D, bytes_accessed=4 * 10 ** 6,
                                      transcendentals=2 * 96 * 256),
    )(recv, send, *sums, *[x.reshape(view.shape) for x in grads], after)


def on_device(queries, key_rows, value_rows, saved_out, logsumexp, out_grad, proj_weight):
    q, k, v = queries[0], key_rows[0], value_rows[0]
    lse = jnp.transpose(logsumexp, (1, 0, 2))
    tok = q.shape[0]
    seq = lax.axis_size("seq")
    rep = lax.axis_size("rep")
    attn, delta, send = front(saved_out[0], out_grad[0], proj_weight, lse, q, k, v, seq)
    recv = lax.all_to_all(send, "seq", 0, 0)
    part = local_level(0, 5, q, k, v, attn, lse, delta)
    mine = sum_terms(recv, part[3])

    def other(x, bit):
        return lax.ppermute(x, "rep", [(i, i ^ bit) for i in range(rep)])

    part = local_level(5, 1, q, k, v, attn, lse, delta, before=part, after=mine)
    pair_sum = add_after(mine, other(mine, 2), part[3])
    outs = last(recv, send, part[3:], part[:3], after=pair_sum)
    all_sum = pair_sum + other(pair_sum, 1)
    projection_gradient = all_sum * (1.0 / math.sqrt(rep * seq * tok))
    return (*[x.reshape(1, tok, D) for x in outs], projection_gradient)


def solution(mesh):
    rows = P("rep", "seq", None)
    return jax.shard_map(
        on_device,
        mesh=mesh,
        in_specs=(rows, rows, rows, rows, P("rep", None, "seq"), rows, P()),
        out_specs=(rows, rows, rows, P("seq", None)),
        check_vma=False,
    )
```

```python
import functools
import math

import jax
import jax.numpy as jnp
from jax import lax
from jax.experimental import pallas as pl
from jax.experimental.pallas import tpu as pltpu
from jax.sharding import PartitionSpec as P

F32 = jnp.float32
BF16 = jnp.bfloat16
DIL = 128
HEADS = 12
HW = 64
D = HEADS * HW
SUB = 16
LOG2E = math.log2(math.e)
SCALE = HW ** -0.5
HALF = D // 2
PART = HEADS // 2
STAT = 2 * HALF
PROJ = STAT + 128
TERM = D + D // 2
MATE = 4
VMEM = 62 * 2 ** 20


def dot(a, b, ca, cb):
    return lax.dot_general(a, b, (((ca,), (cb,)), ((), ())), preferred_element_type=F32)


def iota(shape, axis):
    return lax.broadcasted_iota(jnp.int32, shape, axis)


def head_rows(rows):
    keep = iota((1, SUB, D), 1) == iota((1, SUB, D), 2) // HW
    return jnp.sum(jnp.where(keep, rows.astype(F32), 0.0), axis=1)


def three_terms(x, half):
    x = jnp.where(iota(x.shape, 1) < PART, pltpu.roll(x, 128 - PART, 1) if half else x, 0.0)
    hi = x.astype(BF16).astype(F32)
    mid = (x - hi).astype(BF16).astype(F32)
    low = ((x - hi) - mid).astype(BF16).astype(F32)
    return hi + pltpu.roll(mid, 16, 1) + pltpu.roll(low, 32, 1)


def join_terms(x):
    return (x + pltpu.roll(x, 112, 1)) + pltpu.roll(x, 96, 1)


def front_kernel(steps, seq, saved_ref, grad_ref, w_ref, lse_ref, q_ref, k_ref, v_ref,
                 attn_ref, delta_ref, send_ref, acc, gsel, dsel):
    step = pl.program_id(0)
    saved = saved_ref[...]
    grad = grad_ref[...]
    rows = saved.shape[0]
    attn = dot(grad, w_ref[...], 1, 1).astype(BF16)
    attn_ref[...] = attn
    attn_f = attn.astype(F32)
    term = dot(saved, grad, 0, 0)

    @pl.when(step == 0)
    def _():
        acc[...] = term

    @pl.when(step > 0)
    def _():
        acc[...] += term

    prod = attn_f * saved.astype(F32)
    hi = prod.astype(BF16)
    low = (prod - hi.astype(F32)).astype(BF16)
    pick = (iota((D, 128), 0) // HW == iota((D, 128), 1)).astype(BF16)
    delta = dot(hi, pick, 1, 0) + dot(low, pick, 1, 0)
    delta_ref[...] = delta.T[:SUB]
    groups = rows // DIL
    grouped = attn_f.reshape(groups, DIL, D)[:, :SUB]
    picked = head_rows(grouped)
    diag = iota((1, DIL, 128), 1) == iota((1, DIL, 128), 2)
    dpicked = jnp.sum(jnp.where(diag, delta.reshape(groups, DIL, 128), 0.0), axis=1)
    for i in range(groups):
        gsel[pl.ds(step * groups + i, 1), :] = picked[i:i + 1]
        dsel[pl.ds(step * groups + i, 1), :] = dpicked[i:i + 1]

    @pl.when(step == steps - 1)
    def _():
        lane = iota((1, 128), 1)
        lse = jnp.concatenate(
            [sum(jnp.where(lane == h, lse_ref[h, :, DIL * j:DIL * (j + 1)], 0.0) for h in range(HEADS))
             for j in range(8)], axis=0)
        rows = [head_rows(q_ref[...]), head_rows(k_ref[...]), head_rows(v_ref[...]), gsel[...]]
        own = []
        for half in range(2):
            q, k, v, g = (x[:, HALF * half:HALF * (half + 1)] for x in rows)
            top = jnp.concatenate([q, k, three_terms(lse, half)], axis=1)
            bot = jnp.concatenate([v, g, three_terms(dsel[...], half)], axis=1)
            own.append(jnp.concatenate([top, bot], axis=0).astype(BF16))
        share = D // seq
        for s in range(seq):
            send_ref[s, :, 0:PROJ] = own[1 if s & MATE else 0]
            send_ref[s, :, PROJ:PROJ + D] = acc[share * s:share * s + 16].astype(BF16)
            rest = acc[share * s + 16:share * s + 24]
            send_ref[s, :, PROJ + D:] = jnp.concatenate(
                [rest[:, :D // 2], rest[:, D // 2:]], axis=0).astype(BF16)


def front(saved, grad, w, lse, q, k, v, seq):
    tok = saved.shape[0]
    steps = 4
    rows = tok // steps
    row_spec = pl.BlockSpec((rows, D), lambda i: (i, 0))
    sel_spec = pl.BlockSpec((tok // DIL, SUB, D), lambda i: (0, 0, 0))
    view = lambda x: x.reshape(tok // DIL, DIL, D)
    return pl.pallas_call(
        functools.partial(front_kernel, steps, seq),
        grid=(steps,),
        in_specs=[row_spec, row_spec,
                  pl.BlockSpec((D, D), lambda i: (0, 0)),
                  pl.BlockSpec((HEADS, 1, tok), lambda i: (0, 0, 0)),
                  sel_spec, sel_spec, sel_spec],
        out_specs=[row_spec,
                   pl.BlockSpec((SUB, rows), lambda i: (0, i)),
                   pl.BlockSpec((seq, 16, PROJ + TERM), lambda i: (0, 0, 0))],
        out_shape=[jax.ShapeDtypeStruct((tok, D), BF16),
                   jax.ShapeDtypeStruct((SUB, tok), F32),
                   jax.ShapeDtypeStruct((seq, 16, PROJ + TERM), BF16)],
        scratch_shapes=[pltpu.VMEM((D, D), F32),
                        pltpu.VMEM((tok // DIL, D), F32),
                        pltpu.VMEM((tok // DIL, 128), F32)],
        compiler_params=pltpu.CompilerParams(vmem_limit_bytes=VMEM),
        cost_estimate=pl.CostEstimate(flops=4 * tok * D * D, bytes_accessed=9 * 10 ** 6, transcendentals=0),
    )(saved, grad, w, lse, view(q), view(k), view(v))


def local_kernel(chunk, first, q_ref, k_ref, v_ref, g_ref, lse_ref, delta_ref, *rest):
    dq_ref, dk_ref, dv_ref, sq_ref, sk_ref, sv_ref = rest[-6:]
    pair = first + pl.program_id(0)
    q2, k2, v2, g2 = q_ref[...], k_ref[...], v_ref[...], g_ref[...]
    tok = q2.shape[0]
    lane = iota((1, 128), 1)
    k_turned = k2.T
    zero = jnp.zeros((), BF16)
    qm = [jnp.where(lane < HW, q2, zero), jnp.where(lane >= HW, q2, zero)]
    gm = [jnp.where(lane < HW, g2, zero), jnp.where(lane >= HW, g2, zero)]
    grad_k = grad_v = None
    grad_q = []
    for c in range(tok // chunk):
        part = slice(c * chunk, (c + 1) * chunk)
        turned = []
        for h in range(2):
            qc, gc = qm[h][part], gm[h][part]
            lse = lse_ref[2 * pair + h, :, part] * LOG2E
            delta = delta_ref[pl.ds(2 * pair + h, 1), part]
            prob = jnp.exp2(dot(k2, qc, 1, 1) * (SCALE * LOG2E) - lse)
            dscore = (prob * (dot(v2, gc, 1, 1) - delta)).astype(BF16)
            weight = prob.astype(BF16)
            a, b = dot(dscore, qc, 1, 0), dot(weight, gc, 1, 0)
            grad_k = a if grad_k is None else grad_k + a
            grad_v = b if grad_v is None else grad_v + b
            turned.append(dot(k_turned[HW * h:HW * h + HW], dscore, 1, 0))
        grad_q.append(jnp.concatenate(turned, axis=0).T)
    grad_q = jnp.concatenate(grad_q, axis=0) * SCALE
    grad_k = grad_k * SCALE
    groups = tok // DIL
    keep = iota((1, DIL, 128), 1) == 2 * pair + iota((1, DIL, 128), 2) // HW
    for out, sel, val in ((dq_ref, sq_ref, grad_q), (dk_ref, sk_ref, grad_k), (dv_ref, sv_ref, grad_v)):
        out[...] = val.astype(BF16)
        sel[...] = jnp.sum(jnp.where(keep, val.reshape(groups, DIL, 128), 0.0), axis=1)


def local_level(first, count, q, k, v, g, lse, delta, before=(), after=None):
    tok = q.shape[0]
    col = pl.BlockSpec((tok, 128), lambda i: (0, first + i))
    sel = pl.BlockSpec((tok // DIL, 128), lambda i: (0, first + i))
    extra = list(before) + ([] if after is None else [after])
    return pl.pallas_call(
        functools.partial(local_kernel, 256, first),
        grid=(count,),
        in_specs=[col] * 4 + [pl.BlockSpec((HEADS, 1, tok), lambda i: (0, 0, 0)),
                              pl.BlockSpec((SUB, tok), lambda i: (0, 0))]
        + [pl.BlockSpec(memory_space=pl.ANY)] * len(extra),
        out_specs=[col] * 3 + [sel] * 3,
        out_shape=[jax.ShapeDtypeStruct((tok, D), BF16)] * 3
        + [jax.ShapeDtypeStruct((tok // DIL, D), F32)] * 3,
        input_output_aliases={6 + i: i for i in range(len(before))},
        compiler_params=pltpu.CompilerParams(vmem_limit_bytes=VMEM),
        cost_estimate=pl.CostEstimate(flops=20 * count * tok * tok * HW * 2, bytes_accessed=2 * count * 10 ** 6,
                                      transcendentals=2 * count * tok * tok),
    )(q, k, v, g, lse, delta, *extra)


def dilated_kernel(place, recv_ref, own_ref, mate_ref, after, sum_ref, mine_ref, theirs_ref):
    total = jnp.sum(recv_ref[:, :, PROJ:].astype(F32), axis=0)
    sum_ref[:16] = total[:, :D]
    sum_ref[16:, :D // 2] = total[:8, D:]
    sum_ref[16:, D // 2:] = total[8:, D:]
    every = recv_ref[:, :, :PROJ].astype(F32)
    count = every.shape[0] * 8
    top = every[:, :8].reshape(count, PROJ)
    bot = every[:, 8:].reshape(count, PROJ)
    q, k = top[:, :HALF].astype(BF16), top[:, HALF:STAT].astype(BF16)
    v, g = bot[:, :HALF].astype(BF16), bot[:, HALF:STAT].astype(BF16)
    lse = join_terms(top[:, STAT:]).T[:PART]
    delta = join_terms(bot[:, STAT:]).T[:PART]
    own, mate = own_ref[0].astype(F32), mate_ref[0].astype(F32)
    top = jnp.concatenate([own[:8], mate[:8]], axis=0)
    bot = jnp.concatenate([own[8:], mate[8:]], axis=0)
    own_head = iota((PART, 16, HALF), 0) == iota((PART, 16, HALF), 2) // HW

    def by_head(x):
        return jnp.where(own_head, jnp.broadcast_to(x[None], own_head.shape), 0.0).reshape(PART * 16, HALF).astype(BF16)

    def column(x):
        x = jnp.broadcast_to(join_terms(x)[None], (PART, 16, 128))
        x = jnp.where(iota(x.shape, 0) == iota(x.shape, 2), x, 0.0)
        return jnp.sum(x.reshape(PART * 16, 128), axis=1, keepdims=True)

    def row(x):
        return jnp.broadcast_to(x[:, None], (PART, 16, count)).reshape(PART * 16, count)

    def back(x):
        return jnp.sum(jnp.where(own_head, x.reshape(PART, 16, HALF), 0.0), axis=0)

    def pieces(left_s, right_s, left_p, right_p, lse, delta):
        prob = jnp.exp2(dot(left_s, right_s, 1, 1) * (SCALE * LOG2E) - lse * LOG2E)
        dscore = (prob * (dot(left_p, right_p, 1, 1) - delta)).astype(BF16)
        return prob.astype(BF16), dscore

    _, dscore = pieces(by_head(top[:, :HALF]), k, by_head(bot[:, HALF:STAT]), v,
                       column(top[:, STAT:]), column(bot[:, STAT:]))
    grad_q = back(dot(dscore, k, 1, 0)) * SCALE
    weight, dscore = pieces(by_head(top[:, HALF:STAT]), q, by_head(bot[:, :HALF]), g, row(lse), row(delta))
    grad_k = back(dot(dscore, q, 1, 0)) * SCALE
    grad_v = back(dot(weight, g, 1, 0))
    for i, grad in enumerate((grad_q, grad_k, grad_v)):
        mine_ref[:, HALF * i:HALF * (i + 1)] = grad[:8]
        theirs_ref[:, HALF * i:HALF * (i + 1)] = grad[8:]


def dilated_level(recv, me, after):
    seq, _, width = recv.shape
    place = jnp.stack([me, me ^ MATE]).astype(jnp.int32)
    whole = pl.BlockSpec((8, 3 * HALF), lambda i, p: (0, 0))
    return pl.pallas_call(
        dilated_kernel,
        grid_spec=pltpu.PrefetchScalarGridSpec(
            num_scalar_prefetch=1,
            grid=(1,),
            in_specs=[pl.BlockSpec((seq, 16, width), lambda i, p: (0, 0, 0)),
                      pl.BlockSpec((1, 16, PROJ), lambda i, p: (p[0], 0, 0)),
                      pl.BlockSpec((1, 16, PROJ), lambda i, p: (p[1], 0, 0)),
                      pl.BlockSpec(memory_space=pl.ANY)],
            out_specs=[pl.BlockSpec((24, D), lambda i, p: (0, 0)), whole, whole]),
        out_shape=[jax.ShapeDtypeStruct((24, D), F32)] + [jax.ShapeDtypeStruct((8, 3 * HALF), F32)] * 2,
        compiler_params=pltpu.CompilerParams(vmem_limit_bytes=VMEM),
        cost_estimate=pl.CostEstimate(flops=7 * 2 * 96 * 256 * HALF, bytes_accessed=3 * 10 ** 6,
                                      transcendentals=2 * 96 * 256),
    )(place, recv, recv, recv, after)


def last_kernel(scale, place, mine_ref, theirs_ref, sq_ref, sk_ref, sv_ref, a_ref, b_ref, c_ref, d_ref,
                dq_in, dk_in, dv_in, dq_ref, dk_ref, dv_ref, proj_ref):
    proj_ref[...] = ((a_ref[...] + b_ref[...]) + (c_ref[...] + d_ref[...])) * scale
    first = place[0] == 0
    here = iota((8, SUB, D), 1) == iota((8, SUB, D), 2) // HW
    for i, (sel, old, out) in enumerate(((sq_ref, dq_in, dq_ref), (sk_ref, dk_in, dk_ref), (sv_ref, dv_in, dv_ref))):
        part = slice(HALF * i, HALF * (i + 1))
        mine, theirs = mine_ref[:, part], theirs_ref[:, part]
        total = sel[...] + jnp.concatenate([jnp.where(first, mine, theirs), jnp.where(first, theirs, mine)], axis=1)
        out[...] = jnp.where(here, jnp.broadcast_to(total[:, None], (8, SUB, D)),
                             old[...].astype(F32)).astype(BF16)


def last(me, mine, theirs, sums, terms, grads, scale):
    tok = grads[0].shape[0]
    place = jnp.reshape(me & MATE, (1,)).astype(jnp.int32)
    sub = pl.BlockSpec((tok // DIL, SUB, D), lambda i, p: (0, 0, 0))

    def whole(x):
        return pl.BlockSpec(x.shape, lambda i, p: (0, 0))

    view = jax.ShapeDtypeStruct((tok // DIL, DIL, D), BF16)
    small = (mine, theirs, *sums, *terms)
    return pl.pallas_call(
        functools.partial(last_kernel, scale),
        grid_spec=pltpu.PrefetchScalarGridSpec(
            num_scalar_prefetch=1,
            grid=(1,),
            in_specs=[whole(x) for x in small] + [sub] * 3,
            out_specs=[sub] * 3 + [whole(terms[0])]),
        out_shape=[view] * 3 + [jax.ShapeDtypeStruct(terms[0].shape, F32)],
        input_output_aliases={1 + len(small) + i: i for i in range(3)},
        compiler_params=pltpu.CompilerParams(vmem_limit_bytes=16 * 2 ** 20),
        cost_estimate=pl.CostEstimate(flops=10 ** 6, bytes_accessed=2 * 10 ** 6, transcendentals=0),
    )(place, *small, *[x.reshape(view.shape) for x in grads])


def on_device(queries, key_rows, value_rows, saved_out, logsumexp, out_grad, proj_weight):
    q, k, v = queries[0], key_rows[0], value_rows[0]
    lse = jnp.transpose(logsumexp, (1, 0, 2))
    tok = q.shape[0]
    seq = lax.axis_size("seq")
    rep = lax.axis_size("rep")
    attn, delta, send = front(saved_out[0], out_grad[0], proj_weight, lse, q, k, v, seq)
    recv = lax.all_to_all(send, "seq", 0, 0)
    me = lax.axis_index("seq")
    part = local_level(0, 4, q, k, v, attn, lse, delta)
    term, mine, theirs = dilated_level(recv, me, part[3])

    def other(x, axis, size, bit):
        return lax.ppermute(x, axis, [(i, i ^ bit) for i in range(size)])

    theirs = other(theirs, "seq", seq, MATE)
    terms = (term, *[other(term, "rep", rep, bit) for bit in (2, 1, 3)])
    part = local_level(4, 2, q, k, v, attn, lse, delta, before=part, after=term)
    *outs, projection_gradient = last(me, mine, theirs, part[3:], terms, part[:3], 1.0 / math.sqrt(rep * seq * tok))
    return (*[x.reshape(1, tok, D) for x in outs], projection_gradient)


def solution(mesh):
    rows = P("rep", "seq", None)
    return jax.shard_map(
        on_device,
        mesh=mesh,
        in_specs=(rows, rows, rows, rows, P("rep", None, "seq"), rows, P()),
        out_specs=(rows, rows, rows, P("seq", None)),
        check_vma=False,
    )
```

```python
import functools
import math

import jax
import jax.numpy as jnp
from jax import lax
from jax.experimental import pallas as pl
from jax.experimental.pallas import tpu as pltpu
from jax.sharding import PartitionSpec as P

F32 = jnp.float32
BF16 = jnp.bfloat16
DIL = 128
HEADS = 12
HW = 64
D = HEADS * HW
SUB = 16
LOG2E = math.log2(math.e)
SCALE = HW ** -0.5
HALF = D // 2
PART = HEADS // 2
STAT = 2 * HALF
PROJ = STAT + 128
TERM = D + D // 2
MATE = 4
VMEM = 62 * 2 ** 20


def dot(a, b, ca, cb):
    return lax.dot_general(a, b, (((ca,), (cb,)), ((), ())), preferred_element_type=F32)


def iota(shape, axis):
    return lax.broadcasted_iota(jnp.int32, shape, axis)


def head_rows(rows):
    keep = iota((1, SUB, D), 1) == iota((1, SUB, D), 2) // HW
    return jnp.sum(jnp.where(keep, rows.astype(F32), 0.0), axis=1)


def three_terms(x, half):
    x = jnp.where(iota(x.shape, 1) < PART, pltpu.roll(x, 128 - PART, 1) if half else x, 0.0)
    hi = x.astype(BF16).astype(F32)
    mid = (x - hi).astype(BF16).astype(F32)
    low = ((x - hi) - mid).astype(BF16).astype(F32)
    return hi + pltpu.roll(mid, 16, 1) + pltpu.roll(low, 32, 1)


def join_terms(x):
    return (x + pltpu.roll(x, 112, 1)) + pltpu.roll(x, 96, 1)


def front_kernel(chunks, seq, saved_hbm, grad_hbm, w_hbm, lse_ref, q_hbm, k_hbm, v_hbm,
                 attn_hbm, delta_ref, send_hbm,
                 saved_ref, grad_ref, w_ref, pick_ref, attn_ref, send_ref, acc, in_sems, out_sems):
    tok = saved_ref.shape[0]
    rows = tok // chunks
    groups = rows // DIL
    halves = [pl.ds(i * (tok // 2), tok // 2) for i in range(2)]

    loads = []

    def load(source, target):
        loads.append(pltpu.make_async_copy(source, target, in_sems.at[len(loads)]))
        loads[-1].start()

    for half in halves:
        load(grad_hbm.at[half], grad_ref.at[half])
        load(saved_hbm.at[half], saved_ref.at[half])
    load(w_hbm, w_ref)
    for i, x in enumerate((q_hbm, k_hbm, v_hbm)):
        load(x.at[:, pl.ds(0, SUB)], pick_ref.at[i])

    stores = []

    def store(source, target):
        stores.append(pltpu.make_async_copy(source, target, out_sems.at[len(stores)]))
        stores[-1].start()

    loads[0].wait()
    loads[1].wait()
    acc[...] = dot(saved_ref[halves[0]], grad_ref[halves[0]], 0, 0)
    loads[2].wait()
    loads[3].wait()
    share = D // seq
    for i in range(2):
        wide = slice(HALF * i, HALF * (i + 1))
        term = acc[wide] + dot(saved_ref[halves[1], wide], grad_ref[halves[1]], 0, 0)
        for s in range(seq // 2):
            here = send_ref.at[i * (seq // 2) + s]
            here[:, PROJ:PROJ + D] = term[share * s:share * s + 16].astype(BF16)
            rest = term[share * s + 16:share * s + 24]
            here[:, PROJ + D:] = jnp.concatenate([rest[:, :D // 2], rest[:, D // 2:]], axis=0).astype(BF16)
        some = (pl.ds(i * (seq // 2), seq // 2), slice(None), pl.ds(PROJ, TERM))
        store(send_ref.at[some], send_hbm.at[some])

    loads[4].wait()
    pick = (iota((D, 128), 0) // HW == iota((D, 128), 1)).astype(BF16)
    diag = iota((1, DIL, 128), 1) == iota((1, DIL, 128), 2)
    picked_g, picked_d = [], []
    for c in range(chunks):
        part = pl.ds(c * rows, rows)
        attn = dot(grad_ref[part], w_ref[...], 1, 1).astype(BF16)
        attn_ref[part] = attn
        store(attn_ref.at[part], attn_hbm.at[part])
        attn = attn.astype(F32)
        prod = attn * saved_ref[part].astype(F32)
        hi = prod.astype(BF16)
        low = (prod - hi.astype(F32)).astype(BF16)
        delta = dot(hi, pick, 1, 0) + dot(low, pick, 1, 0)
        delta_ref[:, part] = delta.T[:SUB]
        picked_g.append(head_rows(attn.reshape(groups, DIL, D)[:, :SUB]))
        picked_d.append(jnp.sum(jnp.where(diag, delta.reshape(groups, DIL, 128), 0.0), axis=1))

    for copy in loads[5:]:
        copy.wait()
    lane = iota((1, 128), 1)
    lse = jnp.concatenate(
        [sum(jnp.where(lane == h, lse_ref[h, :, DIL * j:DIL * (j + 1)], 0.0) for h in range(HEADS))
         for j in range(tok // DIL)], axis=0)
    delta = jnp.concatenate(picked_d, axis=0)
    picked = [head_rows(pick_ref[0]), head_rows(pick_ref[1]), head_rows(pick_ref[2]),
              jnp.concatenate(picked_g, axis=0)]
    own = []
    for half in range(2):
        q, k, v, g = (x[:, HALF * half:HALF * (half + 1)] for x in picked)
        top = jnp.concatenate([q, k, three_terms(lse, half)], axis=1)
        bot = jnp.concatenate([v, g, three_terms(delta, half)], axis=1)
        own.append(jnp.concatenate([top, bot], axis=0).astype(BF16))
    for s in range(seq):
        send_ref[s, :, 0:PROJ] = own[1 if s & MATE else 0]
    store(send_ref.at[:, :, pl.ds(0, PROJ)], send_hbm.at[:, :, pl.ds(0, PROJ)])
    for copy in stores:
        copy.wait()


def front(saved, grad, w, lse, q, k, v, seq):
    tok = saved.shape[0]
    chunks = 2
    view = lambda x: x.reshape(tok // DIL, DIL, D)
    anywhere = pl.BlockSpec(memory_space=pl.ANY)
    inside = pl.BlockSpec(memory_space=pltpu.VMEM)
    width = PROJ + TERM
    return pl.pallas_call(
        functools.partial(front_kernel, chunks, seq),
        in_specs=[anywhere, anywhere, anywhere, inside, anywhere, anywhere, anywhere],
        out_specs=[anywhere, inside, anywhere],
        out_shape=[jax.ShapeDtypeStruct((tok, D), BF16),
                   jax.ShapeDtypeStruct((SUB, tok), F32),
                   jax.ShapeDtypeStruct((seq, 16, width), BF16)],
        scratch_shapes=[pltpu.VMEM((tok, D), BF16), pltpu.VMEM((tok, D), BF16), pltpu.VMEM((D, D), BF16),
                        pltpu.VMEM((3, tok // DIL, SUB, D), BF16), pltpu.VMEM((tok, D), BF16),
                        pltpu.VMEM((seq, 16, width), BF16), pltpu.VMEM((D, D), F32),
                        pltpu.SemaphoreType.DMA((8,)), pltpu.SemaphoreType.DMA((chunks + 3,))],
        compiler_params=pltpu.CompilerParams(vmem_limit_bytes=VMEM),
        cost_estimate=pl.CostEstimate(flops=4 * tok * D * D, bytes_accessed=9 * 10 ** 6, transcendentals=0),
    )(saved, grad, w, lse, view(q), view(k), view(v))


def local_kernel(chunk, first, q_ref, k_ref, v_ref, g_ref, lse_ref, delta_ref, *rest):
    dq_ref, dk_ref, dv_ref, sums_ref = rest[-4:]
    pair = first + pl.program_id(0)
    q2, k2, v2, g2 = q_ref[...], k_ref[...], v_ref[...], g_ref[...]
    tok = q2.shape[0]
    lane = iota((1, 128), 1)
    k_turned = k2.T
    zero = jnp.zeros((), BF16)
    qm = [jnp.where(lane < HW, q2, zero), jnp.where(lane >= HW, q2, zero)]
    gm = [jnp.where(lane < HW, g2, zero), jnp.where(lane >= HW, g2, zero)]
    grad_k = grad_v = None
    grad_q = []
    for c in range(tok // chunk):
        part = slice(c * chunk, (c + 1) * chunk)
        turned = []
        for h in range(2):
            qc, gc = qm[h][part], gm[h][part]
            lse = lse_ref[2 * pair + h, :, part] * LOG2E
            delta = delta_ref[pl.ds(2 * pair + h, 1), part]
            prob = jnp.exp2(dot(k2, qc, 1, 1) * (SCALE * LOG2E) - lse)
            dscore = (prob * (dot(v2, gc, 1, 1) - delta)).astype(BF16)
            weight = prob.astype(BF16)
            a, b = dot(dscore, qc, 1, 0), dot(weight, gc, 1, 0)
            grad_k = a if grad_k is None else grad_k + a
            grad_v = b if grad_v is None else grad_v + b
            turned.append(dot(k_turned[HW * h:HW * h + HW], dscore, 1, 0))
        grad_q.append(jnp.concatenate(turned, axis=0).T)
    grad_q = jnp.concatenate(grad_q, axis=0) * SCALE
    grad_k = grad_k * SCALE
    groups = tok // DIL
    keep = iota((1, DIL, 128), 1) == 2 * pair + iota((1, DIL, 128), 2) // HW
    for i, (out, val) in enumerate(((dq_ref, grad_q), (dk_ref, grad_k), (dv_ref, grad_v))):
        out[...] = val.astype(BF16)
        sums_ref[groups * i:groups * (i + 1)] = jnp.sum(
            jnp.where(keep, val.reshape(groups, DIL, 128), 0.0), axis=1)


def local_level(first, count, q, k, v, g, lse, delta, before=(), after=None):
    tok = q.shape[0]
    col = pl.BlockSpec((tok, 128), lambda i: (0, first + i))
    sums = pl.BlockSpec((3 * (tok // DIL), 128), lambda i: (0, first + i))
    extra = list(before) + ([] if after is None else [after])
    return pl.pallas_call(
        functools.partial(local_kernel, 256, first),
        grid=(count,),
        in_specs=[col] * 4 + [pl.BlockSpec((HEADS, 1, tok), lambda i: (0, 0, 0)),
                              pl.BlockSpec((SUB, tok), lambda i: (0, 0))]
        + [pl.BlockSpec(memory_space=pl.ANY)] * len(extra),
        out_specs=[col] * 3 + [sums],
        out_shape=[jax.ShapeDtypeStruct((tok, D), BF16)] * 3
        + [jax.ShapeDtypeStruct((3 * (tok // DIL), D), F32)],
        input_output_aliases={6 + i: i for i in range(len(before))},
        compiler_params=pltpu.CompilerParams(vmem_limit_bytes=VMEM),
        cost_estimate=pl.CostEstimate(flops=20 * count * tok * tok * HW * 2, bytes_accessed=2 * count * 10 ** 6,
                                      transcendentals=2 * count * tok * tok),
    )(q, k, v, g, lse, delta, *extra)


def dilated_kernel(place, recv_hbm, own_ref, mate_ref, after, sum_ref, mine_ref, theirs_ref,
                   rows_ref, terms_ref, sems):
    loads = [pltpu.make_async_copy(recv_hbm.at[:, :, pl.ds(0, PROJ)], rows_ref, sems.at[0]),
             pltpu.make_async_copy(recv_hbm.at[:, :, pl.ds(PROJ, TERM)], terms_ref, sems.at[1])]
    for load in loads:
        load.start()
    loads[0].wait()
    every = rows_ref[...].astype(F32)
    count = every.shape[0] * 8
    top = every[:, :8].reshape(count, PROJ)
    bot = every[:, 8:].reshape(count, PROJ)
    q, k = top[:, :HALF].astype(BF16), top[:, HALF:STAT].astype(BF16)
    v, g = bot[:, :HALF].astype(BF16), bot[:, HALF:STAT].astype(BF16)
    lse = join_terms(top[:, STAT:]).T[:PART]
    delta = join_terms(bot[:, STAT:]).T[:PART]
    own, mate = own_ref[0].astype(F32), mate_ref[0].astype(F32)
    top = jnp.concatenate([own[:8], mate[:8]], axis=0)
    bot = jnp.concatenate([own[8:], mate[8:]], axis=0)
    own_head = iota((PART, 16, HALF), 0) == iota((PART, 16, HALF), 2) // HW

    def by_head(x):
        return jnp.where(own_head, jnp.broadcast_to(x[None], own_head.shape), 0.0).reshape(PART * 16, HALF).astype(BF16)

    def column(x):
        x = jnp.broadcast_to(join_terms(x)[None], (PART, 16, 128))
        x = jnp.where(iota(x.shape, 0) == iota(x.shape, 2), x, 0.0)
        return jnp.sum(x.reshape(PART * 16, 128), axis=1, keepdims=True)

    def row(x):
        return jnp.broadcast_to(x[:, None], (PART, 16, count)).reshape(PART * 16, count)

    def back(x):
        return jnp.sum(jnp.where(own_head, x.reshape(PART, 16, HALF), 0.0), axis=0)

    def pieces(left_s, right_s, left_p, right_p, lse, delta):
        prob = jnp.exp2(dot(left_s, right_s, 1, 1) * (SCALE * LOG2E) - lse * LOG2E)
        dscore = (prob * (dot(left_p, right_p, 1, 1) - delta)).astype(BF16)
        return prob.astype(BF16), dscore

    _, dscore = pieces(by_head(top[:, :HALF]), k, by_head(bot[:, HALF:STAT]), v,
                       column(top[:, STAT:]), column(bot[:, STAT:]))
    grad_q = back(dot(dscore, k, 1, 0)) * SCALE
    weight, dscore = pieces(by_head(top[:, HALF:STAT]), q, by_head(bot[:, :HALF]), g, row(lse), row(delta))
    grad_k = back(dot(dscore, q, 1, 0)) * SCALE
    grad_v = back(dot(weight, g, 1, 0))
    for i, grad in enumerate((grad_q, grad_k, grad_v)):
        mine_ref[:, HALF * i:HALF * (i + 1)] = grad[:8]
        theirs_ref[:, HALF * i:HALF * (i + 1)] = grad[8:]
    loads[1].wait()
    total = jnp.sum(terms_ref[...].astype(F32), axis=0)
    sum_ref[:16] = total[:, :D]
    sum_ref[16:, :D // 2] = total[:8, D:]
    sum_ref[16:, D // 2:] = total[8:, D:]


def dilated_level(recv, me, after):
    seq = recv.shape[0]
    place = jnp.reshape(me, (1,))
    whole = pl.BlockSpec((8, 3 * HALF), lambda i, p: (0, 0))
    return pl.pallas_call(
        dilated_kernel,
        grid_spec=pltpu.PrefetchScalarGridSpec(
            num_scalar_prefetch=1,
            grid=(1,),
            in_specs=[pl.BlockSpec(memory_space=pl.ANY),
                      pl.BlockSpec((1, 16, PROJ), lambda i, p: (p[0], 0, 0)),
                      pl.BlockSpec((1, 16, PROJ), lambda i, p: (p[0] ^ MATE, 0, 0)),
                      pl.BlockSpec(memory_space=pl.ANY)],
            out_specs=[pl.BlockSpec((24, D), lambda i, p: (0, 0)), whole, whole],
            scratch_shapes=[pltpu.VMEM((seq, 16, PROJ), BF16), pltpu.VMEM((seq, 16, TERM), BF16),
                            pltpu.SemaphoreType.DMA((2,))]),
        out_shape=[jax.ShapeDtypeStruct((24, D), F32)] + [jax.ShapeDtypeStruct((8, 3 * HALF), F32)] * 2,
        compiler_params=pltpu.CompilerParams(vmem_limit_bytes=VMEM),
        cost_estimate=pl.CostEstimate(flops=7 * 2 * 96 * 256 * HALF, bytes_accessed=3 * 10 ** 6,
                                      transcendentals=2 * 96 * 256),
    )(place, recv, recv, recv, after)


def last_kernel(scale, place, mine_ref, theirs_ref, sums_ref, a_ref, b_ref, c_ref, d_ref,
                dq_in, dk_in, dv_in, dq_ref, dk_ref, dv_ref, proj_ref):
    proj_ref[...] = ((a_ref[...] + b_ref[...]) + (c_ref[...] + d_ref[...])) * scale
    first = place[0] & MATE == 0
    here = iota((8, SUB, D), 1) == iota((8, SUB, D), 2) // HW
    for i, (old, out) in enumerate(((dq_in, dq_ref), (dk_in, dk_ref), (dv_in, dv_ref))):
        part = slice(HALF * i, HALF * (i + 1))
        mine, theirs = mine_ref[:, part], theirs_ref[:, part]
        total = sums_ref[8 * i:8 * (i + 1)] + jnp.concatenate([jnp.where(first, mine, theirs), jnp.where(first, theirs, mine)], axis=1)
        out[...] = jnp.where(here, jnp.broadcast_to(total[:, None], (8, SUB, D)),
                             old[...].astype(F32)).astype(BF16)


def last(me, mine, theirs, sums, terms, grads, scale):
    tok = grads[0].shape[0]
    place = jnp.reshape(me, (1,))
    sub = pl.BlockSpec((tok // DIL, SUB, D), lambda i, p: (0, 0, 0))

    def whole(x):
        return pl.BlockSpec(x.shape, lambda i, p: (0, 0))

    view = jax.ShapeDtypeStruct((tok // DIL, DIL, D), BF16)
    small = (mine, theirs, sums, *terms)
    return pl.pallas_call(
        functools.partial(last_kernel, scale),
        grid_spec=pltpu.PrefetchScalarGridSpec(
            num_scalar_prefetch=1,
            grid=(1,),
            in_specs=[whole(x) for x in small] + [sub] * 3,
            out_specs=[sub] * 3 + [whole(terms[0])]),
        out_shape=[view] * 3 + [jax.ShapeDtypeStruct(terms[0].shape, F32)],
        input_output_aliases={1 + len(small) + i: i for i in range(3)},
        compiler_params=pltpu.CompilerParams(vmem_limit_bytes=16 * 2 ** 20),
        cost_estimate=pl.CostEstimate(flops=10 ** 6, bytes_accessed=2 * 10 ** 6, transcendentals=0),
    )(place, *small, *[x.reshape(view.shape) for x in grads])


def on_device(queries, key_rows, value_rows, saved_out, logsumexp, out_grad, proj_weight):
    q, k, v = queries[0], key_rows[0], value_rows[0]
    lse = jnp.transpose(logsumexp, (1, 0, 2))
    tok = q.shape[0]
    seq = lax.axis_size("seq")
    rep = lax.axis_size("rep")
    attn, delta, send = front(saved_out[0], out_grad[0], proj_weight, lse, q, k, v, seq)
    recv = lax.all_to_all(send, "seq", 0, 0)
    me = lax.axis_index("seq")
    part = local_level(0, 5, q, k, v, attn, lse, delta)
    term, mine, theirs = dilated_level(recv, me, part[3])

    def other(x, axis, size, bit):
        return lax.ppermute(x, axis, [(i, i ^ bit) for i in range(size)])

    theirs = other(theirs, "seq", seq, MATE)
    terms = (term, *[other(term, "rep", rep, bit) for bit in (2, 1, 3)])
    part = local_level(5, 1, q, k, v, attn, lse, delta, before=part, after=term)
    *outs, projection_gradient = last(me, mine, theirs, part[3], terms, part[:3], 1.0 / math.sqrt(rep * seq * tok))
    return (*[x.reshape(1, tok, D) for x in outs], projection_gradient)


def solution(mesh):
    rows = P("rep", "seq", None)
    return jax.shard_map(
        on_device,
        mesh=mesh,
        in_specs=(rows, rows, rows, rows, P("rep", None, "seq"), rows, P()),
        out_specs=(rows, rows, rows, P("seq", None)),
        check_vma=False,
    )
```

```python
import functools
import math

import jax
import jax.numpy as jnp
from jax import lax
from jax.experimental import pallas as pl
from jax.experimental.pallas import tpu as pltpu
from jax.sharding import PartitionSpec as P

F32 = jnp.float32
BF16 = jnp.bfloat16
DIL = 128
HEADS = 12
HW = 64
D = HEADS * HW
SUB = 16
LOG2E = math.log2(math.e)
SCALE = HW ** -0.5
HALF = D // 2
PART = HEADS // 2
STAT = 2 * HALF
PROJ = STAT + 128
TERM = D + D // 2
MATE = 4
VMEM = 62 * 2 ** 20


def dot(a, b, ca, cb):
    return lax.dot_general(a, b, (((ca,), (cb,)), ((), ())), preferred_element_type=F32)


def iota(shape, axis):
    return lax.broadcasted_iota(jnp.int32, shape, axis)


def head_rows(rows):
    keep = iota((1, SUB, D), 1) == iota((1, SUB, D), 2) // HW
    return jnp.sum(jnp.where(keep, rows.astype(F32), 0.0), axis=1)


def three_terms(x, half):
    x = jnp.where(iota(x.shape, 1) < PART, pltpu.roll(x, 128 - PART, 1) if half else x, 0.0)
    hi = x.astype(BF16).astype(F32)
    mid = (x - hi).astype(BF16).astype(F32)
    low = ((x - hi) - mid).astype(BF16).astype(F32)
    return hi + pltpu.roll(mid, 16, 1) + pltpu.roll(low, 32, 1)


def join_terms(x):
    return (x + pltpu.roll(x, 112, 1)) + pltpu.roll(x, 96, 1)


def front_kernel(seq, saved_hbm, grad_hbm, w_hbm, lse_hbm, q_hbm, k_hbm, v_hbm,
                 attn_hbm, delta_hbm, send_hbm,
                 saved_ref, grad_ref, w_ref, lse_ref, pick_ref, attn_ref, delta_ref, send_ref, acc,
                 in_sems, out_sems):
    tok = saved_ref.shape[0]
    groups = tok // DIL
    halves = [pl.ds(i * (tok // 2), tok // 2) for i in range(2)]

    loads = []

    def load(source, target):
        loads.append(pltpu.make_async_copy(source, target, in_sems.at[len(loads)]))
        loads[-1].start()

    for half in halves:
        load(grad_hbm.at[half], grad_ref.at[half])
        load(saved_hbm.at[half], saved_ref.at[half])
    load(w_hbm, w_ref)
    for i, x in enumerate((q_hbm, k_hbm, v_hbm)):
        load(x.at[:, pl.ds(0, SUB)], pick_ref.at[i])
    load(lse_hbm, lse_ref)

    stores = []

    def store(source, target):
        stores.append(pltpu.make_async_copy(source, target, out_sems.at[len(stores)]))
        stores[-1].start()

    loads[0].wait()
    loads[1].wait()
    acc[...] = dot(saved_ref[halves[0]], grad_ref[halves[0]], 0, 0)
    loads[2].wait()
    loads[3].wait()
    share = D // seq
    for i in range(2):
        wide = slice(HALF * i, HALF * (i + 1))
        term = acc[wide] + dot(saved_ref[halves[1], wide], grad_ref[halves[1]], 0, 0)
        for s in range(seq // 2):
            here = send_ref.at[i * (seq // 2) + s]
            here[:, PROJ:PROJ + D] = term[share * s:share * s + 16].astype(BF16)
            rest = term[share * s + 16:share * s + 24]
            here[:, PROJ + D:] = jnp.concatenate([rest[:, :D // 2], rest[:, D // 2:]], axis=0).astype(BF16)
        some = (pl.ds(i * (seq // 2), seq // 2), slice(None), pl.ds(PROJ, TERM))
        store(send_ref.at[some], send_hbm.at[some])

    loads[4].wait()
    pick = (iota((D, 128), 0) // HW == iota((D, 128), 1)).astype(BF16)
    diag = iota((1, DIL, 128), 1) == iota((1, DIL, 128), 2)
    attn = dot(grad_ref[...], w_ref[...], 1, 1).astype(BF16)
    attn_ref[...] = attn
    store(attn_ref, attn_hbm)
    attn = attn.astype(F32)
    prod = attn * saved_ref[...].astype(F32)
    hi = prod.astype(BF16)
    low = (prod - hi.astype(F32)).astype(BF16)
    delta = dot(hi, pick, 1, 0) + dot(low, pick, 1, 0)
    delta_ref[...] = delta.T[:SUB]
    store(delta_ref, delta_hbm)
    picked_g = head_rows(attn.reshape(groups, DIL, D)[:, :SUB])
    delta = jnp.sum(jnp.where(diag, delta.reshape(groups, DIL, 128), 0.0), axis=1)

    for copy in loads[5:]:
        copy.wait()
    lane = iota((1, 128), 1)
    lse = jnp.concatenate(
        [sum(jnp.where(lane == h, lse_ref[h, :, DIL * j:DIL * (j + 1)], 0.0) for h in range(HEADS))
         for j in range(tok // DIL)], axis=0)
    picked = [head_rows(pick_ref[0]), head_rows(pick_ref[1]), head_rows(pick_ref[2]), picked_g]
    own = []
    for half in range(2):
        q, k, v, g = (x[:, HALF * half:HALF * (half + 1)] for x in picked)
        top = jnp.concatenate([q, k, three_terms(lse, half)], axis=1)
        bot = jnp.concatenate([v, g, three_terms(delta, half)], axis=1)
        own.append(jnp.concatenate([top, bot], axis=0).astype(BF16))
    for s in range(seq):
        send_ref[s, :, 0:PROJ] = own[1 if s & MATE else 0]
    store(send_ref.at[:, :, pl.ds(0, PROJ)], send_hbm.at[:, :, pl.ds(0, PROJ)])
    for copy in stores:
        copy.wait()


def front(saved, grad, w, lse, q, k, v, seq):
    tok = saved.shape[0]
    view = lambda x: x.reshape(tok // DIL, DIL, D)
    anywhere = pl.BlockSpec(memory_space=pl.ANY)
    width = PROJ + TERM
    return pl.pallas_call(
        functools.partial(front_kernel, seq),
        in_specs=[anywhere] * 7,
        out_specs=[anywhere] * 3,
        out_shape=[jax.ShapeDtypeStruct((tok, D), BF16),
                   jax.ShapeDtypeStruct((SUB, tok), F32),
                   jax.ShapeDtypeStruct((seq, 16, width), BF16)],
        scratch_shapes=[pltpu.VMEM((tok, D), BF16), pltpu.VMEM((tok, D), BF16), pltpu.VMEM((D, D), BF16),
                        pltpu.VMEM((HEADS, 1, tok), F32), pltpu.VMEM((3, tok // DIL, SUB, D), BF16),
                        pltpu.VMEM((tok, D), BF16), pltpu.VMEM((SUB, tok), F32),
                        pltpu.VMEM((seq, 16, width), BF16), pltpu.VMEM((D, D), F32),
                        pltpu.SemaphoreType.DMA((9,)), pltpu.SemaphoreType.DMA((5,))],
        compiler_params=pltpu.CompilerParams(vmem_limit_bytes=VMEM),
        cost_estimate=pl.CostEstimate(flops=4 * tok * D * D, bytes_accessed=9 * 10 ** 6, transcendentals=0),
    )(saved, grad, w, lse, view(q), view(k), view(v))


def local_kernel(chunk, first, q_ref, k_ref, v_ref, g_ref, lse_ref, delta_ref, *rest):
    dq_ref, dk_ref, dv_ref, sums_ref = rest[-4:]
    pair = first + pl.program_id(0)
    q2, k2, v2, g2 = q_ref[...], k_ref[...], v_ref[...], g_ref[...]
    tok = q2.shape[0]
    lane = iota((1, 128), 1)
    k_turned = k2.T

    def stacked(x):
        zero = jnp.zeros((), BF16)
        return jnp.concatenate([jnp.where(lane < HW, x, zero), jnp.where(lane >= HW, x, zero)], axis=0)

    def chosen(x):
        return jnp.where(lane < HW, x[:tok], x[tok:])

    k_stack, v_stack = stacked(k2), stacked(v2)
    grad_k = grad_v = None
    grad_q = []
    for c in range(tok // chunk):
        part = slice(c * chunk, (c + 1) * chunk)
        scores = dot(k_stack, q2[part], 1, 1)
        dprobs = dot(v_stack, g2[part], 1, 1)
        dscores, weights, turned = [], [], []
        for h in range(2):
            rows = slice(tok * h, tok * (h + 1))
            lse = lse_ref[2 * pair + h, :, part] * LOG2E
            delta = delta_ref[pl.ds(2 * pair + h, 1), part]
            prob = jnp.exp2(scores[rows] * (SCALE * LOG2E) - lse)
            dscores.append((prob * (dprobs[rows] - delta)).astype(BF16))
            weights.append(prob.astype(BF16))
            turned.append(dot(k_turned[HW * h:HW * h + HW], dscores[h], 1, 0))
        a = dot(jnp.concatenate(dscores, axis=0), q2[part], 1, 0)
        b = dot(jnp.concatenate(weights, axis=0), g2[part], 1, 0)
        grad_k = a if grad_k is None else grad_k + a
        grad_v = b if grad_v is None else grad_v + b
        grad_q.append(jnp.concatenate(turned, axis=0).T)
    grad_q = jnp.concatenate(grad_q, axis=0) * SCALE
    grad_k = chosen(grad_k) * SCALE
    grad_v = chosen(grad_v)
    groups = tok // DIL
    keep = iota((1, DIL, 128), 1) == 2 * pair + iota((1, DIL, 128), 2) // HW
    for i, (out, val) in enumerate(((dq_ref, grad_q), (dk_ref, grad_k), (dv_ref, grad_v))):
        out[...] = val.astype(BF16)
        sums_ref[groups * i:groups * (i + 1)] = jnp.sum(
            jnp.where(keep, val.reshape(groups, DIL, 128), 0.0), axis=1)


def local_level(first, count, q, k, v, g, lse, delta, before=(), after=None):
    tok = q.shape[0]
    col = pl.BlockSpec((tok, 128), lambda i: (0, first + i))
    sums = pl.BlockSpec((3 * (tok // DIL), 128), lambda i: (0, first + i))
    extra = list(before) + ([] if after is None else [after])
    return pl.pallas_call(
        functools.partial(local_kernel, 256, first),
        grid=(count,),
        in_specs=[col] * 4 + [pl.BlockSpec((HEADS, 1, tok), lambda i: (0, 0, 0)),
                              pl.BlockSpec((SUB, tok), lambda i: (0, 0))]
        + [pl.BlockSpec(memory_space=pl.ANY)] * len(extra),
        out_specs=[col] * 3 + [sums],
        out_shape=[jax.ShapeDtypeStruct((tok, D), BF16)] * 3
        + [jax.ShapeDtypeStruct((3 * (tok // DIL), D), F32)],
        input_output_aliases={6 + i: i for i in range(len(before))},
        compiler_params=pltpu.CompilerParams(vmem_limit_bytes=VMEM),
        cost_estimate=pl.CostEstimate(flops=20 * count * tok * tok * HW * 2, bytes_accessed=2 * count * 10 ** 6,
                                      transcendentals=2 * count * tok * tok),
    )(q, k, v, g, lse, delta, *extra)


def dilated_kernel(place, recv_hbm, after, sum_ref, mine_ref, theirs_ref,
                   rows_ref, terms_ref, sems):
    loads = [pltpu.make_async_copy(recv_hbm.at[:, :, pl.ds(0, PROJ)], rows_ref, sems.at[0]),
             pltpu.make_async_copy(recv_hbm.at[:, :, pl.ds(PROJ, TERM)], terms_ref, sems.at[1])]
    for load in loads:
        load.start()
    loads[0].wait()
    every = rows_ref[...].astype(F32)
    count = every.shape[0] * 8
    top = every[:, :8].reshape(count, PROJ)
    bot = every[:, 8:].reshape(count, PROJ)
    q, k = top[:, :HALF].astype(BF16), top[:, HALF:STAT].astype(BF16)
    v, g = bot[:, :HALF].astype(BF16), bot[:, HALF:STAT].astype(BF16)
    lse = join_terms(top[:, STAT:]).T[:PART]
    delta = join_terms(bot[:, STAT:]).T[:PART]
    own, mate = rows_ref[place[0]].astype(F32), rows_ref[place[0] ^ MATE].astype(F32)
    top = jnp.concatenate([own[:8], mate[:8]], axis=0)
    bot = jnp.concatenate([own[8:], mate[8:]], axis=0)
    own_head = iota((PART, 16, HALF), 0) == iota((PART, 16, HALF), 2) // HW

    def by_head(x):
        return jnp.where(own_head, jnp.broadcast_to(x[None], own_head.shape), 0.0).reshape(PART * 16, HALF).astype(BF16)

    def column(x):
        x = jnp.broadcast_to(join_terms(x)[None], (PART, 16, 128))
        x = jnp.where(iota(x.shape, 0) == iota(x.shape, 2), x, 0.0)
        return jnp.sum(x.reshape(PART * 16, 128), axis=1, keepdims=True)

    def row(x):
        return jnp.broadcast_to(x[:, None], (PART, 16, count)).reshape(PART * 16, count)

    def back(x):
        return jnp.sum(jnp.where(own_head, x.reshape(PART, 16, HALF), 0.0), axis=0)

    def pieces(left_s, right_s, left_p, right_p, lse, delta):
        prob = jnp.exp2(dot(left_s, right_s, 1, 1) * (SCALE * LOG2E) - lse * LOG2E)
        dscore = (prob * (dot(left_p, right_p, 1, 1) - delta)).astype(BF16)
        return prob.astype(BF16), dscore

    _, dscore = pieces(by_head(top[:, :HALF]), k, by_head(bot[:, HALF:STAT]), v,
                       column(top[:, STAT:]), column(bot[:, STAT:]))
    grad_q = back(dot(dscore, k, 1, 0)) * SCALE
    weight, dscore = pieces(by_head(top[:, HALF:STAT]), q, by_head(bot[:, :HALF]), g, row(lse), row(delta))
    grad_k = back(dot(dscore, q, 1, 0)) * SCALE
    grad_v = back(dot(weight, g, 1, 0))
    for i, grad in enumerate((grad_q, grad_k, grad_v)):
        mine_ref[:, HALF * i:HALF * (i + 1)] = grad[:8]
        theirs_ref[:, HALF * i:HALF * (i + 1)] = grad[8:]
    loads[1].wait()
    total = jnp.sum(terms_ref[...].astype(F32), axis=0)
    sum_ref[:16] = total[:, :D]
    sum_ref[16:, :D // 2] = total[:8, D:]
    sum_ref[16:, D // 2:] = total[8:, D:]


def dilated_level(recv, me, after):
    seq = recv.shape[0]
    place = jnp.reshape(me, (1,))
    whole = pl.BlockSpec((8, 3 * HALF), lambda i, p: (0, 0))
    return pl.pallas_call(
        dilated_kernel,
        grid_spec=pltpu.PrefetchScalarGridSpec(
            num_scalar_prefetch=1,
            grid=(1,),
            in_specs=[pl.BlockSpec(memory_space=pl.ANY)] * 2,
            out_specs=[pl.BlockSpec((24, D), lambda i, p: (0, 0)), whole, whole],
            scratch_shapes=[pltpu.VMEM((seq, 16, PROJ), BF16), pltpu.VMEM((seq, 16, TERM), BF16),
                            pltpu.SemaphoreType.DMA((2,))]),
        out_shape=[jax.ShapeDtypeStruct((24, D), F32)] + [jax.ShapeDtypeStruct((8, 3 * HALF), F32)] * 2,
        compiler_params=pltpu.CompilerParams(vmem_limit_bytes=VMEM),
        cost_estimate=pl.CostEstimate(flops=7 * 2 * 96 * 256 * HALF, bytes_accessed=3 * 10 ** 6,
                                      transcendentals=2 * 96 * 256),
    )(place, recv, after)


def last_kernel(scale, place, mine_ref, theirs_ref, a_ref, b_ref, c_ref, d_ref, sums_hbm,
                dq_in, dk_in, dv_in, dq_ref, dk_ref, dv_ref, proj_ref, sums_ref, sem):
    load = pltpu.make_async_copy(sums_hbm, sums_ref, sem)
    load.start()
    proj_ref[...] = ((a_ref[...] + b_ref[...]) + (c_ref[...] + d_ref[...])) * scale
    first = place[0] & MATE == 0
    here = iota((8, SUB, D), 1) == iota((8, SUB, D), 2) // HW
    load.wait()
    for i, (old, out) in enumerate(((dq_in, dq_ref), (dk_in, dk_ref), (dv_in, dv_ref))):
        part = slice(HALF * i, HALF * (i + 1))
        mine, theirs = mine_ref[:, part], theirs_ref[:, part]
        total = sums_ref[8 * i:8 * (i + 1)] + jnp.concatenate([jnp.where(first, mine, theirs), jnp.where(first, theirs, mine)], axis=1)
        out[...] = jnp.where(here, jnp.broadcast_to(total[:, None], (8, SUB, D)),
                             old[...].astype(F32)).astype(BF16)


def last(me, mine, theirs, sums, terms, grads, scale):
    tok = grads[0].shape[0]
    place = jnp.reshape(me, (1,))
    sub = pl.BlockSpec((tok // DIL, SUB, D), lambda i, p: (0, 0, 0))

    def whole(x):
        return pl.BlockSpec(x.shape, lambda i, p: (0, 0))

    view = jax.ShapeDtypeStruct((tok // DIL, DIL, D), BF16)
    small = (mine, theirs, *terms)
    return pl.pallas_call(
        functools.partial(last_kernel, scale),
        grid_spec=pltpu.PrefetchScalarGridSpec(
            num_scalar_prefetch=1,
            grid=(1,),
            in_specs=[whole(x) for x in small] + [pl.BlockSpec(memory_space=pl.ANY)] + [sub] * 3,
            out_specs=[sub] * 3 + [whole(terms[0])],
            scratch_shapes=[pltpu.VMEM(sums.shape, F32), pltpu.SemaphoreType.DMA(())]),
        out_shape=[view] * 3 + [jax.ShapeDtypeStruct(terms[0].shape, F32)],
        input_output_aliases={2 + len(small) + i: i for i in range(3)},
        compiler_params=pltpu.CompilerParams(vmem_limit_bytes=16 * 2 ** 20),
        cost_estimate=pl.CostEstimate(flops=10 ** 6, bytes_accessed=2 * 10 ** 6, transcendentals=0),
    )(place, *small, sums, *[x.reshape(view.shape) for x in grads])


def on_device(queries, key_rows, value_rows, saved_out, logsumexp, out_grad, proj_weight):
    q, k, v = queries[0], key_rows[0], value_rows[0]
    lse = jnp.transpose(logsumexp, (1, 0, 2))
    tok = q.shape[0]
    seq = lax.axis_size("seq")
    rep = lax.axis_size("rep")
    attn, delta, send = front(saved_out[0], out_grad[0], proj_weight, lse, q, k, v, seq)
    recv = lax.all_to_all(send, "seq", 0, 0)
    me = lax.axis_index("seq")
    part = local_level(0, 5, q, k, v, attn, lse, delta)
    term, mine, theirs = dilated_level(recv, me, part[3])

    def other(x, axis, size, bit):
        return lax.ppermute(x, axis, [(i, i ^ bit) for i in range(size)])

    theirs = other(theirs, "seq", seq, MATE)
    terms = (term, *[other(term, "rep", rep, bit) for bit in (2, 1, 3)])
    part = local_level(5, 1, q, k, v, attn, lse, delta, before=part, after=term)
    *outs, projection_gradient = last(me, mine, theirs, part[3], terms, part[:3], 1.0 / math.sqrt(rep * seq * tok))
    return (*[x.reshape(1, tok, D) for x in outs], projection_gradient)


def solution(mesh):
    rows = P("rep", "seq", None)
    return jax.shard_map(
        on_device,
        mesh=mesh,
        in_specs=(rows, rows, rows, rows, P("rep", None, "seq"), rows, P()),
        out_specs=(rows, rows, rows, P("seq", None)),
        check_vma=False,
    )
```

```python
import functools
import math

import jax
import jax.numpy as jnp
from jax import lax
from jax.experimental import pallas as pl
from jax.experimental.pallas import tpu as pltpu
from jax.sharding import PartitionSpec as P

F32 = jnp.float32
BF16 = jnp.bfloat16
DIL = 128
HEADS = 12
HW = 64
D = HEADS * HW
SUB = 16
LOG2E = math.log2(math.e)
SCALE = HW ** -0.5
HALF = D // 2
PART = HEADS // 2
STAT = 2 * HALF
PROJ = STAT + 128
TERM = D + D // 2
MATE = 4
VMEM = 62 * 2 ** 20
ROOM = 4096


def dot(a, b, ca, cb):
    return lax.dot_general(a, b, (((ca,), (cb,)), ((), ())), preferred_element_type=F32)


def iota(shape, axis):
    return lax.broadcasted_iota(jnp.int32, shape, axis)


def head_rows(rows):
    keep = iota((1, SUB, D), 1) == iota((1, SUB, D), 2) // HW
    return jnp.sum(jnp.where(keep, rows.astype(F32), 0.0), axis=1)


def three_terms(x, half):
    x = jnp.where(iota(x.shape, 1) < PART, pltpu.roll(x, 128 - PART, 1) if half else x, 0.0)
    hi = x.astype(BF16).astype(F32)
    mid = (x - hi).astype(BF16).astype(F32)
    low = ((x - hi) - mid).astype(BF16).astype(F32)
    return hi + pltpu.roll(mid, 16, 1) + pltpu.roll(low, 32, 1)


def join_terms(x):
    return (x + pltpu.roll(x, 112, 1)) + pltpu.roll(x, 96, 1)


def front_kernel(seq, saved_hbm, grad_hbm, w_hbm, lse_hbm, q_hbm, k_hbm, v_hbm,
                 attn_hbm, delta_hbm, send_hbm,
                 saved_ref, grad_ref, w_ref, lse_ref, pick_ref, attn_ref, delta_ref, send_ref,
                 in_sems, out_sems):
    tok = saved_ref.shape[0]
    groups = tok // DIL

    loads = []

    def load(source, target):
        loads.append(pltpu.make_async_copy(source, target, in_sems.at[len(loads)]))
        loads[-1].start()

    load(grad_hbm, grad_ref)
    load(saved_hbm, saved_ref)
    load(w_hbm, w_ref)
    for i, x in enumerate((q_hbm, k_hbm, v_hbm)):
        load(x.at[:, pl.ds(0, SUB)], pick_ref.at[i])
    load(lse_hbm, lse_ref)

    stores = []

    def store(source, target):
        stores.append(pltpu.make_async_copy(source, target, out_sems.at[len(stores)]))
        stores[-1].start()

    for copy in loads:
        copy.wait()
    pick = (iota((D, 128), 0) // HW == iota((D, 128), 1)).astype(BF16)
    diag = iota((1, DIL, 128), 1) == iota((1, DIL, 128), 2)
    attn = dot(grad_ref[...], w_ref[...], 1, 1).astype(BF16)
    attn_ref[...] = attn
    attn = attn.astype(F32)
    prod = attn * saved_ref[...].astype(F32)
    hi = prod.astype(BF16)
    low = (prod - hi.astype(F32)).astype(BF16)
    delta = dot(hi, pick, 1, 0) + dot(low, pick, 1, 0)
    delta_ref[...] = delta.T[:SUB]
    store(attn_ref, attn_hbm)
    store(delta_ref, delta_hbm)
    picked_g = head_rows(attn.reshape(groups, DIL, D)[:, :SUB])
    delta = jnp.sum(jnp.where(diag, delta.reshape(groups, DIL, 128), 0.0), axis=1)

    lane = iota((1, 128), 1)
    lse = jnp.concatenate(
        [sum(jnp.where(lane == h, lse_ref[h, :, DIL * j:DIL * (j + 1)], 0.0) for h in range(HEADS))
         for j in range(tok // DIL)], axis=0)
    picked = [head_rows(pick_ref[0]), head_rows(pick_ref[1]), head_rows(pick_ref[2]), picked_g]
    own = []
    for half in range(2):
        q, k, v, g = (x[:, HALF * half:HALF * (half + 1)] for x in picked)
        top = jnp.concatenate([q, k, three_terms(lse, half)], axis=1)
        bot = jnp.concatenate([v, g, three_terms(delta, half)], axis=1)
        own.append(jnp.concatenate([top, bot], axis=0).astype(BF16))
    for s in range(seq):
        send_ref[s, :, 0:PROJ] = own[1 if s & MATE else 0]
    store(send_ref.at[:, :, pl.ds(0, PROJ)], send_hbm.at[:, :, pl.ds(0, PROJ)])
    share = D // seq
    for i in range(2):
        wide = slice(HALF * i, HALF * (i + 1))
        term = dot(saved_ref[:, wide], grad_ref[...], 0, 0)
        for s in range(seq // 2):
            here = send_ref.at[i * (seq // 2) + s]
            here[:, PROJ:PROJ + D] = term[share * s:share * s + 16].astype(BF16)
            rest = term[share * s + 16:share * s + 24]
            here[:, PROJ + D:] = jnp.concatenate([rest[:, :D // 2], rest[:, D // 2:]], axis=0).astype(BF16)
        some = (pl.ds(i * (seq // 2), seq // 2), slice(None), pl.ds(PROJ, TERM))
        store(send_ref.at[some], send_hbm.at[some])

    for copy in stores:
        copy.wait()


def front(saved, grad, w, lse, q, k, v, seq):
    tok = saved.shape[0]
    view = lambda x: x.reshape(tok // DIL, DIL, D)
    anywhere = pl.BlockSpec(memory_space=pl.ANY)
    width = PROJ + TERM
    return pl.pallas_call(
        functools.partial(front_kernel, seq),
        in_specs=[anywhere] * 7,
        out_specs=[anywhere] * 3,
        out_shape=[jax.ShapeDtypeStruct((tok, D), BF16),
                   jax.ShapeDtypeStruct((SUB, tok), F32),
                   jax.ShapeDtypeStruct((seq, 16, width), BF16)],
        scratch_shapes=[pltpu.VMEM((tok, D), BF16), pltpu.VMEM((tok, D), BF16), pltpu.VMEM((D, D), BF16),
                        pltpu.VMEM((HEADS, 1, tok), F32), pltpu.VMEM((3, tok // DIL, SUB, D), BF16),
                        pltpu.VMEM((tok, D), BF16), pltpu.VMEM((SUB, tok), F32),
                        pltpu.VMEM((seq, 16, width), BF16),
                        pltpu.SemaphoreType.DMA((7,)), pltpu.SemaphoreType.DMA((5,))],
        compiler_params=pltpu.CompilerParams(vmem_limit_bytes=VMEM),
        cost_estimate=pl.CostEstimate(flops=4 * tok * D * D, bytes_accessed=9 * 10 ** 6, transcendentals=0),
    )(saved, grad, w, lse, view(q), view(k), view(v))


def local_kernel(chunk, first, q_ref, k_ref, v_ref, g_ref, lse_ref, delta_ref, *rest):
    dq_ref, dk_ref, dv_ref, sums_ref = rest[-4:]
    pair = first + pl.program_id(0)
    q2, k2, v2, g2 = q_ref[...], k_ref[...], v_ref[...], g_ref[...]
    tok = q2.shape[0]
    lane = iota((1, 128), 1)
    k_turned = k2.T

    def stacked(x):
        zero = jnp.zeros((), BF16)
        return jnp.concatenate([jnp.where(lane < HW, x, zero), jnp.where(lane >= HW, x, zero)], axis=0)

    def chosen(x):
        return jnp.where(lane < HW, x[:tok], x[tok:])

    k_stack, v_stack = stacked(k2), stacked(v2)
    grad_k = grad_v = None
    grad_q = []
    for c in range(tok // chunk):
        part = slice(c * chunk, (c + 1) * chunk)
        scores = dot(k_stack, q2[part], 1, 1)
        dprobs = dot(v_stack, g2[part], 1, 1)
        dscores, weights, turned = [], [], []
        for h in range(2):
            rows = slice(tok * h, tok * (h + 1))
            lse = lse_ref[2 * pair + h, :, part] * LOG2E
            delta = delta_ref[pl.ds(2 * pair + h, 1), part]
            prob = jnp.exp2(scores[rows] * (SCALE * LOG2E) - lse)
            dscores.append((prob * (dprobs[rows] - delta)).astype(BF16))
            weights.append(prob.astype(BF16))
            turned.append(dot(k_turned[HW * h:HW * h + HW], dscores[h], 1, 0))
        a = dot(jnp.concatenate(dscores, axis=0), q2[part], 1, 0)
        b = dot(jnp.concatenate(weights, axis=0), g2[part], 1, 0)
        grad_k = a if grad_k is None else grad_k + a
        grad_v = b if grad_v is None else grad_v + b
        grad_q.append(jnp.concatenate(turned, axis=0).T)
    grad_q = jnp.concatenate(grad_q, axis=0) * SCALE
    grad_k = chosen(grad_k) * SCALE
    grad_v = chosen(grad_v)
    groups = tok // DIL
    keep = iota((1, DIL, 128), 1) == 2 * pair + iota((1, DIL, 128), 2) // HW
    for i, (out, val) in enumerate(((dq_ref, grad_q), (dk_ref, grad_k), (dv_ref, grad_v))):
        out[...] = val.astype(BF16)
        sums_ref[groups * i:groups * (i + 1)] = jnp.sum(
            jnp.where(keep, val.reshape(groups, DIL, 128), 0.0), axis=1)


def local_level(first, count, q, k, v, g, lse, delta, before=(), after=None):
    tok = q.shape[0]
    col = pl.BlockSpec((tok, 128), lambda i: (0, first + i))
    sums = pl.BlockSpec((3 * (tok // DIL), 128), lambda i: (0, first + i))
    extra = list(before) + ([] if after is None else [after])
    return pl.pallas_call(
        functools.partial(local_kernel, 256, first),
        grid=(count,),
        in_specs=[col] * 4 + [pl.BlockSpec((HEADS, 1, tok), lambda i: (0, 0, 0)),
                              pl.BlockSpec((SUB, tok), lambda i: (0, 0))]
        + [pl.BlockSpec(memory_space=pl.ANY)] * len(extra),
        out_specs=[col] * 3 + [sums],
        out_shape=[jax.ShapeDtypeStruct((tok, D), BF16)] * 3
        + [jax.ShapeDtypeStruct((ROOM, D), F32)],
        input_output_aliases={6 + i: i for i in range(len(before))},
        compiler_params=pltpu.CompilerParams(vmem_limit_bytes=VMEM),
        cost_estimate=pl.CostEstimate(flops=20 * count * tok * tok * HW * 2, bytes_accessed=2 * count * 10 ** 6,
                                      transcendentals=2 * count * tok * tok),
    )(q, k, v, g, lse, delta, *extra)


def dilated_kernel(place, recv_hbm, after, sum_ref, mine_ref, theirs_ref,
                   rows_ref, terms_ref, sems):
    loads = [pltpu.make_async_copy(recv_hbm.at[:, :, pl.ds(0, PROJ)], rows_ref, sems.at[0]),
             pltpu.make_async_copy(recv_hbm.at[:, :, pl.ds(PROJ, TERM)], terms_ref, sems.at[1])]
    for load in loads:
        load.start()
    loads[0].wait()
    every = rows_ref[...].astype(F32)
    count = every.shape[0] * 8
    top = every[:, :8].reshape(count, PROJ)
    bot = every[:, 8:].reshape(count, PROJ)
    q, k = top[:, :HALF].astype(BF16), top[:, HALF:STAT].astype(BF16)
    v, g = bot[:, :HALF].astype(BF16), bot[:, HALF:STAT].astype(BF16)
    lse = join_terms(top[:, STAT:]).T[:PART]
    delta = join_terms(bot[:, STAT:]).T[:PART]
    own, mate = rows_ref[place[0]].astype(F32), rows_ref[place[0] ^ MATE].astype(F32)
    top = jnp.concatenate([own[:8], mate[:8]], axis=0)
    bot = jnp.concatenate([own[8:], mate[8:]], axis=0)
    own_head = iota((PART, 16, HALF), 0) == iota((PART, 16, HALF), 2) // HW

    def by_head(x):
        return jnp.where(own_head, jnp.broadcast_to(x[None], own_head.shape), 0.0).reshape(PART * 16, HALF).astype(BF16)

    def column(x):
        x = jnp.broadcast_to(join_terms(x)[None], (PART, 16, 128))
        x = jnp.where(iota(x.shape, 0) == iota(x.shape, 2), x, 0.0)
        return jnp.sum(x.reshape(PART * 16, 128), axis=1, keepdims=True)

    def row(x):
        return jnp.broadcast_to(x[:, None], (PART, 16, count)).reshape(PART * 16, count)

    def back(x):
        return jnp.sum(jnp.where(own_head, x.reshape(PART, 16, HALF), 0.0), axis=0)

    def pieces(left_s, right_s, left_p, right_p, lse, delta):
        prob = jnp.exp2(dot(left_s, right_s, 1, 1) * (SCALE * LOG2E) - lse * LOG2E)
        dscore = (prob * (dot(left_p, right_p, 1, 1) - delta)).astype(BF16)
        return prob.astype(BF16), dscore

    _, dscore = pieces(by_head(top[:, :HALF]), k, by_head(bot[:, HALF:STAT]), v,
                       column(top[:, STAT:]), column(bot[:, STAT:]))
    grad_q = back(dot(dscore, k, 1, 0)) * SCALE
    weight, dscore = pieces(by_head(top[:, HALF:STAT]), q, by_head(bot[:, :HALF]), g, row(lse), row(delta))
    grad_k = back(dot(dscore, q, 1, 0)) * SCALE
    grad_v = back(dot(weight, g, 1, 0))
    for i, grad in enumerate((grad_q, grad_k, grad_v)):
        mine_ref[:, HALF * i:HALF * (i + 1)] = grad[:8]
        theirs_ref[:, HALF * i:HALF * (i + 1)] = grad[8:]
    loads[1].wait()
    total = jnp.sum(terms_ref[...].astype(F32), axis=0)
    sum_ref[:16] = total[:, :D]
    sum_ref[16:, :D // 2] = total[:8, D:]
    sum_ref[16:, D // 2:] = total[8:, D:]


def dilated_level(recv, me, after):
    seq = recv.shape[0]
    place = jnp.reshape(me, (1,))
    whole = pl.BlockSpec((8, 3 * HALF), lambda i, p: (0, 0))
    return pl.pallas_call(
        dilated_kernel,
        grid_spec=pltpu.PrefetchScalarGridSpec(
            num_scalar_prefetch=1,
            grid=(1,),
            in_specs=[pl.BlockSpec(memory_space=pl.ANY)] * 2,
            out_specs=[pl.BlockSpec((24, D), lambda i, p: (0, 0)), whole, whole],
            scratch_shapes=[pltpu.VMEM((seq, 16, PROJ), BF16), pltpu.VMEM((seq, 16, TERM), BF16),
                            pltpu.SemaphoreType.DMA((2,))]),
        out_shape=[jax.ShapeDtypeStruct((24, D), F32)] + [jax.ShapeDtypeStruct((8, 3 * HALF), F32)] * 2,
        compiler_params=pltpu.CompilerParams(vmem_limit_bytes=VMEM),
        cost_estimate=pl.CostEstimate(flops=7 * 2 * 96 * 256 * HALF, bytes_accessed=3 * 10 ** 6,
                                      transcendentals=2 * 96 * 256),
    )(place, recv, after)


def last_kernel(scale, place, mine_ref, theirs_ref, a_ref, b_ref, c_ref, d_ref, sums_ref,
                dq_in, dk_in, dv_in, dq_ref, dk_ref, dv_ref, proj_ref):
    proj_ref[...] = ((a_ref[...] + b_ref[...]) + (c_ref[...] + d_ref[...])) * scale
    first = place[0] & MATE == 0
    here = iota((8, SUB, D), 1) == iota((8, SUB, D), 2) // HW
    for i, (old, out) in enumerate(((dq_in, dq_ref), (dk_in, dk_ref), (dv_in, dv_ref))):
        part = slice(HALF * i, HALF * (i + 1))
        mine, theirs = mine_ref[:, part], theirs_ref[:, part]
        total = sums_ref[8 * i:8 * (i + 1)] + jnp.concatenate([jnp.where(first, mine, theirs), jnp.where(first, theirs, mine)], axis=1)
        out[...] = jnp.where(here, jnp.broadcast_to(total[:, None], (8, SUB, D)),
                             old[...].astype(F32)).astype(BF16)


def last(me, mine, theirs, sums, terms, grads, scale):
    tok = grads[0].shape[0]
    place = jnp.reshape(me, (1,))
    sub = pl.BlockSpec((tok // DIL, SUB, D), lambda i, p: (0, 0, 0))

    def whole(x):
        return pl.BlockSpec(x.shape, lambda i, p: (0, 0))

    view = jax.ShapeDtypeStruct((tok // DIL, DIL, D), BF16)
    small = (mine, theirs, *terms)
    return pl.pallas_call(
        functools.partial(last_kernel, scale),
        grid_spec=pltpu.PrefetchScalarGridSpec(
            num_scalar_prefetch=1,
            grid=(1,),
            in_specs=[whole(x) for x in small] + [pl.BlockSpec((3 * (tok // DIL), D), lambda i, p: (0, 0))] + [sub] * 3,
            out_specs=[sub] * 3 + [whole(terms[0])]),
        out_shape=[view] * 3 + [jax.ShapeDtypeStruct(terms[0].shape, F32)],
        input_output_aliases={2 + len(small) + i: i for i in range(3)},
        compiler_params=pltpu.CompilerParams(vmem_limit_bytes=48 * 2 ** 20),
        cost_estimate=pl.CostEstimate(flops=10 ** 6, bytes_accessed=2 * 10 ** 6, transcendentals=0),
    )(place, *small, sums, *[x.reshape(view.shape) for x in grads])


def on_device(queries, key_rows, value_rows, saved_out, logsumexp, out_grad, proj_weight):
    q, k, v = queries[0], key_rows[0], value_rows[0]
    lse = jnp.transpose(logsumexp, (1, 0, 2))
    tok = q.shape[0]
    seq = lax.axis_size("seq")
    rep = lax.axis_size("rep")
    attn, delta, send = front(saved_out[0], out_grad[0], proj_weight, lse, q, k, v, seq)
    recv = lax.all_to_all(send, "seq", 0, 0)
    me = lax.axis_index("seq")
    part = local_level(0, 5, q, k, v, attn, lse, delta)
    term, mine, theirs = dilated_level(recv, me, part[3])

    def other(x, axis, size, bit):
        return lax.ppermute(x, axis, [(i, i ^ bit) for i in range(size)])

    theirs = other(theirs, "seq", seq, MATE)
    terms = (term, *[other(term, "rep", rep, bit) for bit in (2, 1, 3)])
    part = local_level(5, 1, q, k, v, attn, lse, delta, before=part, after=term)
    *outs, projection_gradient = last(me, mine, theirs, part[3], terms, part[:3], 1.0 / math.sqrt(rep * seq * tok))
    return (*[x.reshape(1, tok, D) for x in outs], projection_gradient)


def solution(mesh):
    rows = P("rep", "seq", None)
    return jax.shard_map(
        on_device,
        mesh=mesh,
        in_specs=(rows, rows, rows, rows, P("rep", None, "seq"), rows, P()),
        out_specs=(rows, rows, rows, P("seq", None)),
        check_vma=False,
    )
```

```python
import functools
import math

import jax
import jax.numpy as jnp
from jax import lax
from jax.experimental import pallas as pl
from jax.experimental.pallas import tpu as pltpu
from jax.sharding import PartitionSpec as P

F32 = jnp.float32
BF16 = jnp.bfloat16
DIL = 128
HEADS = 12
HW = 64
D = HEADS * HW
SUB = 16
LOG2E = math.log2(math.e)
SCALE = HW ** -0.5
HALF = D // 2
PART = HEADS // 2
STAT = 2 * HALF
PROJ = STAT + 128
TERM = D + D // 2
MATE = 4
VMEM = 62 * 2 ** 20
ROOM = 8192


def dot(a, b, ca, cb):
    return lax.dot_general(a, b, (((ca,), (cb,)), ((), ())), preferred_element_type=F32)


def iota(shape, axis):
    return lax.broadcasted_iota(jnp.int32, shape, axis)


def head_rows(rows):
    keep = iota((1, SUB, D), 1) == iota((1, SUB, D), 2) // HW
    return jnp.sum(jnp.where(keep, rows.astype(F32), 0.0), axis=1)


def three_terms(x, half):
    x = jnp.where(iota(x.shape, 1) < PART, pltpu.roll(x, 128 - PART, 1) if half else x, 0.0)
    hi = x.astype(BF16).astype(F32)
    mid = (x - hi).astype(BF16).astype(F32)
    low = ((x - hi) - mid).astype(BF16).astype(F32)
    return hi + pltpu.roll(mid, 16, 1) + pltpu.roll(low, 32, 1)


def join_terms(x):
    return (x + pltpu.roll(x, 112, 1)) + pltpu.roll(x, 96, 1)


def front_kernel(seq, saved_hbm, grad_hbm, w_hbm, lse_hbm, q_hbm, k_hbm, v_hbm,
                 attn_hbm, delta_hbm, send_hbm,
                 saved_ref, grad_ref, w_ref, lse_ref, pick_ref, attn_ref, delta_ref, send_ref,
                 in_sems, out_sems):
    tok = saved_ref.shape[0]
    groups = tok // DIL

    loads = []

    def load(source, target):
        loads.append(pltpu.make_async_copy(source, target, in_sems.at[len(loads)]))
        loads[-1].start()

    load(grad_hbm, grad_ref)
    load(saved_hbm, saved_ref)
    load(w_hbm, w_ref)
    for i, x in enumerate((q_hbm, k_hbm, v_hbm)):
        load(x.at[:, pl.ds(0, SUB)], pick_ref.at[i])
    load(lse_hbm, lse_ref)

    stores = []

    def store(source, target):
        stores.append(pltpu.make_async_copy(source, target, out_sems.at[len(stores)]))
        stores[-1].start()

    for copy in loads:
        copy.wait()
    pick = (iota((D, 128), 0) // HW == iota((D, 128), 1)).astype(BF16)
    diag = iota((1, DIL, 128), 1) == iota((1, DIL, 128), 2)
    attn = dot(grad_ref[...], w_ref[...], 1, 1).astype(BF16)
    attn_ref[...] = attn
    attn = attn.astype(F32)
    prod = attn * saved_ref[...].astype(F32)
    hi = prod.astype(BF16)
    low = (prod - hi.astype(F32)).astype(BF16)
    delta = dot(hi, pick, 1, 0) + dot(low, pick, 1, 0)
    delta_ref[...] = delta.T[:SUB]
    store(attn_ref, attn_hbm)
    store(delta_ref, delta_hbm)
    picked_g = head_rows(attn.reshape(groups, DIL, D)[:, :SUB])
    delta = jnp.sum(jnp.where(diag, delta.reshape(groups, DIL, 128), 0.0), axis=1)

    lane = iota((1, 128), 1)
    lse = jnp.concatenate(
        [sum(jnp.where(lane == h, lse_ref[h, :, DIL * j:DIL * (j + 1)], 0.0) for h in range(HEADS))
         for j in range(tok // DIL)], axis=0)
    picked = [head_rows(pick_ref[0]), head_rows(pick_ref[1]), head_rows(pick_ref[2]), picked_g]
    own = []
    for half in range(2):
        q, k, v, g = (x[:, HALF * half:HALF * (half + 1)] for x in picked)
        top = jnp.concatenate([q, k, three_terms(lse, half)], axis=1)
        bot = jnp.concatenate([v, g, three_terms(delta, half)], axis=1)
        own.append(jnp.concatenate([top, bot], axis=0).astype(BF16))
    for s in range(seq):
        send_ref[s, :, 0:PROJ] = own[1 if s & MATE else 0]
    store(send_ref.at[:, :, pl.ds(0, PROJ)], send_hbm.at[:, :, pl.ds(0, PROJ)])
    share = D // seq
    for i in range(2):
        wide = slice(HALF * i, HALF * (i + 1))
        term = dot(saved_ref[:, wide], grad_ref[...], 0, 0)
        for s in range(seq // 2):
            here = send_ref.at[i * (seq // 2) + s]
            here[:, PROJ:PROJ + D] = term[share * s:share * s + 16].astype(BF16)
            rest = term[share * s + 16:share * s + 24]
            here[:, PROJ + D:] = jnp.concatenate([rest[:, :D // 2], rest[:, D // 2:]], axis=0).astype(BF16)
        some = (pl.ds(i * (seq // 2), seq // 2), slice(None), pl.ds(PROJ, TERM))
        store(send_ref.at[some], send_hbm.at[some])

    for copy in stores:
        copy.wait()


def front(saved, grad, w, lse, q, k, v, seq):
    tok = saved.shape[0]
    view = lambda x: x.reshape(tok // DIL, DIL, D)
    anywhere = pl.BlockSpec(memory_space=pl.ANY)
    width = PROJ + TERM
    return pl.pallas_call(
        functools.partial(front_kernel, seq),
        in_specs=[anywhere] * 7,
        out_specs=[anywhere] * 3,
        out_shape=[jax.ShapeDtypeStruct((tok, D), BF16),
                   jax.ShapeDtypeStruct((SUB, tok), F32),
                   jax.ShapeDtypeStruct((seq, 16, width), BF16)],
        scratch_shapes=[pltpu.VMEM((tok, D), BF16), pltpu.VMEM((tok, D), BF16), pltpu.VMEM((D, D), BF16),
                        pltpu.VMEM((HEADS, 1, tok), F32), pltpu.VMEM((3, tok // DIL, SUB, D), BF16),
                        pltpu.VMEM((tok, D), BF16), pltpu.VMEM((SUB, tok), F32),
                        pltpu.VMEM((seq, 16, width), BF16),
                        pltpu.SemaphoreType.DMA((7,)), pltpu.SemaphoreType.DMA((5,))],
        compiler_params=pltpu.CompilerParams(vmem_limit_bytes=VMEM),
        cost_estimate=pl.CostEstimate(flops=4 * tok * D * D, bytes_accessed=9 * 10 ** 6, transcendentals=0),
    )(saved, grad, w, lse, view(q), view(k), view(v))


def local_kernel(chunk, first, q_ref, k_ref, v_ref, g_ref, lse_ref, delta_ref, *rest):
    dq_ref, dk_ref, dv_ref, sums_ref = rest[-4:]
    pair = first + pl.program_id(0)
    q2, k2, v2, g2 = q_ref[...], k_ref[...], v_ref[...], g_ref[...]
    tok = q2.shape[0]
    lane = iota((1, 128), 1)
    k_turned = k2.T

    def stacked(x):
        zero = jnp.zeros((), BF16)
        return jnp.concatenate([jnp.where(lane < HW, x, zero), jnp.where(lane >= HW, x, zero)], axis=0)

    def chosen(x):
        return jnp.where(lane < HW, x[:tok], x[tok:])

    k_stack, v_stack = stacked(k2), stacked(v2)
    grad_k = grad_v = None
    grad_q = []
    for c in range(tok // chunk):
        part = slice(c * chunk, (c + 1) * chunk)
        scores = dot(k_stack, q2[part], 1, 1)
        dprobs = dot(v_stack, g2[part], 1, 1)
        dscores, weights = [], []
        for h in range(2):
            rows = slice(tok * h, tok * (h + 1))
            lse = lse_ref[2 * pair + h, :, part] * LOG2E
            delta = delta_ref[pl.ds(2 * pair + h, 1), part]
            prob = jnp.exp2(scores[rows] * (SCALE * LOG2E) - lse)
            dscores.append((prob * (dprobs[rows] - delta)).astype(BF16))
            weights.append(prob.astype(BF16))
        a = dot(jnp.concatenate(dscores, axis=0), q2[part], 1, 0)
        b = dot(jnp.concatenate(weights, axis=0), g2[part], 1, 0)
        grad_k = a if grad_k is None else grad_k + a
        grad_v = b if grad_v is None else grad_v + b
        turned = [dot(k_turned[HW * h:HW * h + HW], dscores[h], 1, 0) for h in range(2)]
        grad_q.append(jnp.concatenate(turned, axis=0).T)
    grad_q = jnp.concatenate(grad_q, axis=0) * SCALE
    grad_k = chosen(grad_k) * SCALE
    grad_v = chosen(grad_v)
    groups = tok // DIL
    keep = iota((1, DIL, 128), 1) == 2 * pair + iota((1, DIL, 128), 2) // HW
    for i, (out, val) in enumerate(((dq_ref, grad_q), (dk_ref, grad_k), (dv_ref, grad_v))):
        out[...] = val.astype(BF16)
        sums_ref[groups * i:groups * (i + 1)] = jnp.sum(
            jnp.where(keep, val.reshape(groups, DIL, 128), 0.0), axis=1)


def local_level(first, count, q, k, v, g, lse, delta, before=(), after=None, limit=56):
    tok = q.shape[0]
    col = pl.BlockSpec((tok, 128), lambda i: (0, first + i))
    sums = pl.BlockSpec((3 * (tok // DIL), 128), lambda i: (0, first + i))
    extra = list(before) + ([] if after is None else [after])
    return pl.pallas_call(
        functools.partial(local_kernel, 256, first),
        grid=(count,),
        in_specs=[col] * 4 + [pl.BlockSpec((HEADS, 1, tok), lambda i: (0, 0, 0)),
                              pl.BlockSpec((SUB, tok), lambda i: (0, 0))]
        + [pl.BlockSpec(memory_space=pl.ANY)] * len(extra),
        out_specs=[col] * 3 + [sums],
        out_shape=[jax.ShapeDtypeStruct((tok, D), BF16)] * 3
        + [jax.ShapeDtypeStruct((ROOM, D), F32)],
        input_output_aliases={6 + i: i for i in range(len(before))},
        compiler_params=pltpu.CompilerParams(vmem_limit_bytes=limit * 2 ** 20),
        cost_estimate=pl.CostEstimate(flops=20 * count * tok * tok * HW * 2, bytes_accessed=2 * count * 10 ** 6,
                                      transcendentals=2 * count * tok * tok),
    )(q, k, v, g, lse, delta, *extra)


def dilated_kernel(place, recv_hbm, after, sum_ref, mine_ref, theirs_ref,
                   rows_ref, terms_ref, sems):
    loads = [pltpu.make_async_copy(recv_hbm.at[:, :, pl.ds(0, PROJ)], rows_ref, sems.at[0]),
             pltpu.make_async_copy(recv_hbm.at[:, :, pl.ds(PROJ, TERM)], terms_ref, sems.at[1])]
    for load in loads:
        load.start()
    loads[0].wait()
    every = rows_ref[...].astype(F32)
    count = every.shape[0] * 8
    top = every[:, :8].reshape(count, PROJ)
    bot = every[:, 8:].reshape(count, PROJ)
    q, k = top[:, :HALF].astype(BF16), top[:, HALF:STAT].astype(BF16)
    v, g = bot[:, :HALF].astype(BF16), bot[:, HALF:STAT].astype(BF16)
    lse = join_terms(top[:, STAT:]).T[:PART]
    delta = join_terms(bot[:, STAT:]).T[:PART]
    own, mate = rows_ref[place[0]].astype(F32), rows_ref[place[0] ^ MATE].astype(F32)
    top = jnp.concatenate([own[:8], mate[:8]], axis=0)
    bot = jnp.concatenate([own[8:], mate[8:]], axis=0)
    own_head = iota((PART, 16, HALF), 0) == iota((PART, 16, HALF), 2) // HW

    def by_head(x):
        return jnp.where(own_head, jnp.broadcast_to(x[None], own_head.shape), 0.0).reshape(PART * 16, HALF).astype(BF16)

    def column(x):
        x = jnp.broadcast_to(join_terms(x)[None], (PART, 16, 128))
        x = jnp.where(iota(x.shape, 0) == iota(x.shape, 2), x, 0.0)
        return jnp.sum(x.reshape(PART * 16, 128), axis=1, keepdims=True)

    def row(x):
        return jnp.broadcast_to(x[:, None], (PART, 16, count)).reshape(PART * 16, count)

    def back(x):
        return jnp.sum(jnp.where(own_head, x.reshape(PART, 16, HALF), 0.0), axis=0)

    def pieces(left_s, right_s, left_p, right_p, lse, delta):
        prob = jnp.exp2(dot(left_s, right_s, 1, 1) * (SCALE * LOG2E) - lse * LOG2E)
        dscore = (prob * (dot(left_p, right_p, 1, 1) - delta)).astype(BF16)
        return prob.astype(BF16), dscore

    _, dscore = pieces(by_head(top[:, :HALF]), k, by_head(bot[:, HALF:STAT]), v,
                       column(top[:, STAT:]), column(bot[:, STAT:]))
    grad_q = back(dot(dscore, k, 1, 0)) * SCALE
    weight, dscore = pieces(by_head(top[:, HALF:STAT]), q, by_head(bot[:, :HALF]), g, row(lse), row(delta))
    grad_k = back(dot(dscore, q, 1, 0)) * SCALE
    grad_v = back(dot(weight, g, 1, 0))
    for i, grad in enumerate((grad_q, grad_k, grad_v)):
        mine_ref[:, HALF * i:HALF * (i + 1)] = grad[:8]
        theirs_ref[:, HALF * i:HALF * (i + 1)] = grad[8:]
    loads[1].wait()
    total = jnp.sum(terms_ref[...].astype(F32), axis=0)
    sum_ref[:16] = total[:, :D]
    sum_ref[16:, :D // 2] = total[:8, D:]
    sum_ref[16:, D // 2:] = total[8:, D:]


def dilated_level(recv, me, after):
    seq = recv.shape[0]
    place = jnp.reshape(me, (1,))
    whole = pl.BlockSpec((8, 3 * HALF), lambda i, p: (0, 0))
    return pl.pallas_call(
        dilated_kernel,
        grid_spec=pltpu.PrefetchScalarGridSpec(
            num_scalar_prefetch=1,
            grid=(1,),
            in_specs=[pl.BlockSpec(memory_space=pl.ANY)] * 2,
            out_specs=[pl.BlockSpec((24, D), lambda i, p: (0, 0)), whole, whole],
            scratch_shapes=[pltpu.VMEM((seq, 16, PROJ), BF16), pltpu.VMEM((seq, 16, TERM), BF16),
                            pltpu.SemaphoreType.DMA((2,))]),
        out_shape=[jax.ShapeDtypeStruct((24, D), F32)] + [jax.ShapeDtypeStruct((8, 3 * HALF), F32)] * 2,
        compiler_params=pltpu.CompilerParams(vmem_limit_bytes=40 * 2 ** 20),
        cost_estimate=pl.CostEstimate(flops=7 * 2 * 96 * 256 * HALF, bytes_accessed=3 * 10 ** 6,
                                      transcendentals=2 * 96 * 256),
    )(place, recv, after)


def last_kernel(scale, place, mine_ref, theirs_ref, a_ref, b_ref, c_ref, d_ref, sums_ref,
                dq_in, dk_in, dv_in, dq_ref, dk_ref, dv_ref, proj_ref):
    proj_ref[...] = ((a_ref[...] + b_ref[...]) + (c_ref[...] + d_ref[...])) * scale
    first = place[0] & MATE == 0
    here = iota((8, SUB, D), 1) == iota((8, SUB, D), 2) // HW
    for i, (old, out) in enumerate(((dq_in, dq_ref), (dk_in, dk_ref), (dv_in, dv_ref))):
        part = slice(HALF * i, HALF * (i + 1))
        mine, theirs = mine_ref[:, part], theirs_ref[:, part]
        total = sums_ref[8 * i:8 * (i + 1)] + jnp.concatenate([jnp.where(first, mine, theirs), jnp.where(first, theirs, mine)], axis=1)
        out[...] = jnp.where(here, jnp.broadcast_to(total[:, None], (8, SUB, D)),
                             old[...].astype(F32)).astype(BF16)


def last(me, mine, theirs, sums, terms, grads, scale):
    tok = grads[0].shape[0]
    place = jnp.reshape(me, (1,))
    sub = pl.BlockSpec((tok // DIL, SUB, D), lambda i, p: (0, 0, 0))

    def whole(x):
        return pl.BlockSpec(x.shape, lambda i, p: (0, 0))

    view = jax.ShapeDtypeStruct((tok // DIL, DIL, D), BF16)
    small = (mine, theirs, *terms)
    return pl.pallas_call(
        functools.partial(last_kernel, scale),
        grid_spec=pltpu.PrefetchScalarGridSpec(
            num_scalar_prefetch=1,
            grid=(1,),
            in_specs=[whole(x) for x in small] + [pl.BlockSpec((3 * (tok // DIL), D), lambda i, p: (0, 0))] + [sub] * 3,
            out_specs=[sub] * 3 + [whole(terms[0])]),
        out_shape=[view] * 3 + [jax.ShapeDtypeStruct(terms[0].shape, F32)],
        input_output_aliases={2 + len(small) + i: i for i in range(3)},
        compiler_params=pltpu.CompilerParams(vmem_limit_bytes=48 * 2 ** 20),
        cost_estimate=pl.CostEstimate(flops=10 ** 6, bytes_accessed=2 * 10 ** 6, transcendentals=0),
    )(place, *small, sums, *[x.reshape(view.shape) for x in grads])


def on_device(queries, key_rows, value_rows, saved_out, logsumexp, out_grad, proj_weight):
    q, k, v = queries[0], key_rows[0], value_rows[0]
    lse = jnp.transpose(logsumexp, (1, 0, 2))
    tok = q.shape[0]
    seq = lax.axis_size("seq")
    rep = lax.axis_size("rep")
    attn, delta, send = front(saved_out[0], out_grad[0], proj_weight, lse, q, k, v, seq)
    recv = lax.all_to_all(send, "seq", 0, 0)
    me = lax.axis_index("seq")
    part = local_level(0, 5, q, k, v, attn, lse, delta)
    term, mine, theirs = dilated_level(recv, me, part[3])

    def other(x, axis, size, bit):
        return lax.ppermute(x, axis, [(i, i ^ bit) for i in range(size)])

    theirs = other(theirs, "seq", seq, MATE)
    terms = (term, *[other(term, "rep", rep, bit) for bit in (2, 1, 3)])
    part = local_level(5, 1, q, k, v, attn, lse, delta, before=part, after=term, limit=40)
    *outs, projection_gradient = last(me, mine, theirs, part[3], terms, part[:3], 1.0 / math.sqrt(rep * seq * tok))
    return (*[x.reshape(1, tok, D) for x in outs], projection_gradient)


def solution(mesh):
    rows = P("rep", "seq", None)
    return jax.shard_map(
        on_device,
        mesh=mesh,
        in_specs=(rows, rows, rows, rows, P("rep", None, "seq"), rows, P()),
        out_specs=(rows, rows, rows, P("seq", None)),
        check_vma=False,
    )
```
